128 devices in a mesh: region: 16 (over x_lo, z, core), seq: 8 (over x_hi, y).
Axes of the slice: x: 4 (x_hi: 2, x_lo: 2; x = x_hi * 2 + x_lo), y: 4, z: 4, core: 2. Of those that a mesh axis runs over, the one named last changes fastest.
Arguments:
- tokens: bfloat16 [16384, 3584], P(('region', 'seq')), may hold values from -6 to 6
- preact: bfloat16 [16384, 10240], P('region', 'seq'), may hold values from -8 to 8
- cotangent: bfloat16 [16384, 10240], P('region', 'seq'), may hold values from -6 to 6
- master: float32 [3584, 10240], P('region', 'seq'), may hold values from -6 to 6
- first_moment: float32 [3584, 10240], P('region', 'seq'), may hold values from -1.5 to 1.5
- second_moment: float32 [3584, 10240], P('region', 'seq'), may hold values from 0.001 to 0.1
Outputs:
- new_master: float32 [3584, 10240], P('region', 'seq')
- new_first: float32 [3584, 10240], P('region', 'seq')
- new_second: float32 [3584, 10240], P('region', 'seq')
- input_grad: bfloat16 [16384, 3584], P(('region', 'seq'))
The draws below stay inside these ranges and needn't reach their ends.
All inputs are finite; a program needn't handle non-finite values.
Results may differ from the reference program's by a relative error of at most 0.015.
Values may be sent and summed in bfloat16 or wider, within the bound.
A program may use at most 128 MiB of HBM per device.

```python
import math
import jax
import jax.numpy as jnp
from jax import lax

D = 3584
FF = 10240
TOK_DEV = 128
TOKENS = 16384
N_REGION = 16
N_SEQ = 8


def block_levels(key, shape, shards, least, top_value):
    loudness = 1.0
    for position, parts in shards:
        draws = jax.random.uniform(jax.random.fold_in(jax.random.fold_in(key, 6), position), (parts,), jnp.float32, least / len(shards), top_value / len(shards))
        loudness = loudness * jnp.repeat(jnp.exp(draws), shape[position] // parts).reshape((-1,) + (1,) * (len(shape) - 1 - position))
    return loudness


def scatter_about(own_key, shape, width, bound, split=(), kind=jnp.bfloat16):
    gain = block_levels(own_key, shape, split, -0.22, 0.18) if split else 1.0
    result = jax.random.normal(own_key, shape, jnp.float32) * width * gain
    return jnp.minimum(jnp.maximum(result, -bound), bound).astype(kind)


def setup_inputs(seed: int = 0) -> dict:
    streams_of = jax.random.split(jax.random.key(seed), 7)
    tokens = scatter_about(streams_of[0], (TOKENS, D), 1.0, 6.0, ((0, 128),))
    preact = scatter_about(streams_of[1], (TOKENS, FF), 1.5, 8.0, ((0, 16), (1, 8)))
    cotangent = scatter_about(streams_of[2], (TOKENS, FF), 1.0, 6.0, ((0, 16), (1, 8)))
    master = scatter_about(streams_of[3], (D, FF), 1.0, 6.0, ((0, 16), (1, 8)), jnp.float32)
    first_moment = scatter_about(streams_of[4], (D, FF), 0.1, 1.5, ((0, 16), (1, 8)), jnp.float32)
    second_moment = jnp.clip(jnp.exp(math.log(0.1) - 4.6051702 * jax.random.uniform(streams_of[5], (D, FF), jnp.float32) ** block_levels(streams_of[5], (D, FF), ((0, 16), (1, 8)), -0.2, 0.2)), 0.001, 0.1)
    return dict(tokens=tokens, preact=preact, cotangent=cotangent, master=master, first_moment=first_moment, second_moment=second_moment)


def reference(tokens, preact, cotangent, master, first_moment, second_moment):
    linear = preact.astype(jnp.float32)
    sigma = jax.nn.sigmoid(linear)
    slope = (cotangent.astype(jnp.float32) * sigma * (1.0 + linear * (1.0 - sigma))).astype(jnp.bfloat16)
    weights = master.astype(jnp.bfloat16)
    scale = D ** (-0.5)
    region_rows = TOK_DEV * N_SEQ
    block = FF // N_SEQ

    def one_region(index, carry):
        summed, gradient_in = carry
        start = (index * region_rows).astype(jnp.int32)
        inputs = lax.dynamic_slice_in_dim(tokens, start, region_rows, 0)
        slopes = lax.dynamic_slice_in_dim(slope, start, region_rows, 0)
        term = jnp.dot(inputs.T, slopes, preferred_element_type=jnp.float32).astype(jnp.bfloat16)
        term = lax.optimization_barrier(term)
        summed = summed + term.astype(jnp.float32)
        total = jnp.zeros((region_rows, D), jnp.float32)
        for column in range(N_SEQ):
            part = jnp.dot(slopes[:, column * block:(column + 1) * block], weights[:, column * block:(column + 1) * block].T, preferred_element_type=jnp.float32) * scale
            part = lax.optimization_barrier(part.astype(jnp.bfloat16))
            total = total + part.astype(jnp.float32)
        gradient_in = lax.dynamic_update_slice_in_dim(gradient_in, total.astype(jnp.bfloat16), start, 0)
        return (summed, gradient_in)
    summed = jnp.zeros((D, FF), jnp.float32)
    gradient_in = jnp.zeros((TOKENS, D), jnp.bfloat16)
    summed, gradient_in = lax.fori_loop(0, N_REGION, one_region, (summed, gradient_in))
    pseudo = summed * TOKENS ** (-0.5)
    new_first = 0.9 * first_moment + 0.1 * pseudo
    new_second = 0.999 * second_moment + 0.001 * pseudo * pseudo
    new_master = master - 0.1 * new_first / (jnp.sqrt(new_second) + 0.001)
    return (new_master, new_first, new_second, gradient_in)
```

```python
import jax
import jax.numpy as jnp
from jax import lax
from jax.experimental import pallas as pl
from jax.experimental.pallas import tpu as pltpu
from jax.sharding import PartitionSpec as P

MESH = pl.DeviceIdType.MESH
BF = jnp.bfloat16
F32 = jnp.float32

D = 3584
REGIONS = 16
SEQS = 8
OWN = D // REGIONS
CH = 7
RB = OWN // CH
CD = D // CH
TOK = 128
HID = 1280
RT = TOK * SEQS
STAGE = 128


def place(d0):
    owner, rest = divmod(d0, OWN)
    k, i = divmod(rest, RB)
    xl, z, c = owner // 8, owner // 2 % 4, owner % 2
    return k, ((c * 2 + xl) * 4 + z) * RB + i


def rcopy(src, dst, send, recv, dev):
    return pltpu.make_async_remote_copy(
        src_ref=src, dst_ref=dst, send_sem=send, recv_sem=recv, device_id=dev, device_id_type=MESH
    )


def kernel(
    tok, pre, cot, mas, sum_out, ig_out,
    tg, wg, slope, tb, cr, zf, zn, xlb, ib, yf, yn, xhb, tokv, masv, prev, cotv,
    in_sem, st_sem, ts, tr, ws, wr, us, ur, vs, vr,
):
    r = lax.axis_index("region")
    s = lax.axis_index("seq")
    xl, z, c = r // 8, (r // 2) % 4, r % 2
    xh, y = s // 4, s % 4
    ol, oh = 1 - xl, 1 - xh
    zp, zm, zo = (z + 1) % 4, (z + 3) % 4, (z + 2) % 4
    yp, ym, yo = (y + 1) % 4, (y + 3) % 4, (y + 2) % 4

    def rdev(a, b, d):
        return (a * 8 + b * 2 + d, s)

    def sdev(a, b):
        return (r, a * 4 + b)

    d_core = rdev(xl, z, 1 - c)
    d_xl = rdev(ol, z, c)
    d_zp = rdev(xl, zp, c)
    d_zm = rdev(xl, zm, c)
    d_xh = sdev(oh, y)
    d_yp = sdev(xh, yp)
    d_ym = sdev(xh, ym)

    get_tok = pltpu.make_async_copy(tok, tokv, in_sem.at[0])
    get_mas = pltpu.make_async_copy(mas, masv, in_sem.at[1])
    get_tok.start()
    get_mas.start()

    def stage(i, slot):
        rows = pl.ds(pl.multiple_of(i * STAGE, STAGE), STAGE)
        return (
            pltpu.make_async_copy(pre.at[rows], prev.at[slot], st_sem.at[0, slot]),
            pltpu.make_async_copy(cot.at[rows], cotv.at[slot], st_sem.at[1, slot]),
        )

    for i in range(2):
        for copy in stage(i, i):
            copy.start()

    barrier = pltpu.get_barrier_semaphore()
    for dev in (d_core, d_xl, d_zp, d_zm, d_xh, d_yp, d_ym):
        pl.semaphore_signal(barrier, inc=1, device_id=dev, device_id_type=MESH)

    get_tok.wait()
    for j in range(D // 128):
        turned = tokv[:, j * 128:(j + 1) * 128].T
        for m in range(128 // RB):
            k, row = place(j * 128 + m * RB)
            tg[k, s, row:row + RB, :] = turned[m * RB:(m + 1) * RB, :]
    get_mas.wait()
    w_own = xl * 4 + z
    w_oth = ol * 4 + z

    def cast(k, carry):
        wg[k, c, w_own] = masv[k].astype(BF)
        return carry

    lax.fori_loop(0, CH, cast, 0)
    pl.semaphore_wait(barrier, 7)

    def t_copy(k, slot, i, j, dev):
        return rcopy(tg.at[k, slot], tg.at[k, slot], ts.at[k, i], tr.at[k, j], dev)

    def w_copy(k, slot, i, j, dev):
        return rcopy(wg.at[k, c, slot], wg.at[k, c, slot], ws.at[k, i], wr.at[k, j], dev)

    def w_core(k):
        return rcopy(wg.at[k, c], wg.at[k, c], ws.at[k, 7], wr.at[k, 7], d_core)

    def gather0(k, carry):
        t_copy(k, s, 0, 0, d_xh).start()
        t_copy(k, s, 1, 1 + xh, d_yp).start()
        t_copy(k, s, 2, 3 + xh, d_ym).start()
        w_copy(k, w_own, 0, 0, d_xl).start()
        w_copy(k, w_own, 1, 1 + xl, d_zp).start()
        w_copy(k, w_own, 2, 3 + xl, d_zm).start()
        return carry

    def t_wait(k, slot, j):
        t_copy(k, slot, 0, j, d_xh).wait_recv()

    def w_wait(k, slot, j):
        w_copy(k, slot, 0, j, d_xl).wait_recv()

    def gather1(k):
        t_wait(k, oh * 4 + y, 0)
        t_copy(k, oh * 4 + y, 3, 1 + oh, d_yp).start()
        t_copy(k, oh * 4 + y, 4, 3 + oh, d_ym).start()
        w_wait(k, w_oth, 0)
        w_copy(k, w_oth, 3, 1 + ol, d_zp).start()
        w_copy(k, w_oth, 4, 3 + ol, d_zm).start()

    def gather2(k):
        t_wait(k, ym, 1)
        t_copy(k, ym, 5, 5, d_yp).start()
        t_wait(k, 4 + yp, 4)
        t_copy(k, 4 + yp, 6, 6, d_ym).start()
        w_wait(k, zm, 1)
        w_copy(k, zm, 5, 5, d_zp).start()
        w_wait(k, 4 + zp, 4)
        w_copy(k, 4 + zp, 6, 6, d_zm).start()

    def gather3(k):
        w_wait(k, 4 + zm, 2)
        w_wait(k, zp, 3)
        w_wait(k, zo, 5)
        w_wait(k, 4 + zo, 6)
        w_core(k).start()
        t_wait(k, 4 + ym, 2)
        t_wait(k, yp, 3)
        t_wait(k, yo, 5)
        t_wait(k, 4 + yo, 6)

    def u_core(k):
        return rcopy(tb.at[k, 1 - c], cr.at[k], us.at[k, 0], ur.at[k, 0], d_core)

    def u_far(k, p):
        slot = (zo, 4 + zo)[p]
        return rcopy(tb.at[k, c, slot], zf.at[k, p], us.at[k, 1 + p], ur.at[k, 1 + p], (d_zp, d_zm)[p])

    def u_near(k, p, a):
        slot = (zp, zm)[p] + 4 * a
        i = 3 + 2 * p + a
        return rcopy(tb.at[k, c, slot], zn.at[k, p, a], us.at[k, i], ur.at[k, i], (d_zp, d_zm)[p])

    def u_last(k):
        return rcopy(tb.at[k, c, w_oth], xlb.at[k], us.at[k, 7], ur.at[k, 7], d_xl)

    def v_far(k, p):
        slot = (yo, 4 + yo)[p]
        return rcopy(ib.at[k, slot], yf.at[k, p], vs.at[k, 1 + p], vr.at[k, 1 + p], (d_yp, d_ym)[p])

    def v_near(k, p, a):
        slot = (yp, ym)[p] + 4 * a
        i = 3 + 2 * p + a
        return rcopy(ib.at[k, slot], yn.at[k, p, a], vs.at[k, i], vr.at[k, i], (d_yp, d_ym)[p])

    def v_last(k):
        return rcopy(ib.at[k, oh * 4 + y], xhb.at[k], vs.at[k, 7], vr.at[k, 7], d_xh)

    def multiply(k):
        def term(j, carry):
            cols = pl.ds(pl.multiple_of(j * 256, 256), 256)
            left = jnp.concatenate([tg[k, i] for i in range(SEQS)], axis=1)
            out = jnp.dot(left, slope[:, cols], preferred_element_type=F32)
            tb[k, :, :, :, cols] = out.astype(BF).reshape(2, 8, RB, 256)
            return carry

        lax.fori_loop(0, HID // 256, term, 0)
        u_core(k).start()
        rcopy(wg.at[k, 1 - c], wg.at[k, 1 - c], ws.at[k, 7], wr.at[k, 7], d_core).wait_recv()

        def part(j, carry):
            rows = pl.ds(pl.multiple_of(j * 256, 256), 256)
            left = wg[k].reshape(CD, HID)
            out = lax.dot_general(
                left, slope[rows, :], (((1,), (1,)), ((), ())), preferred_element_type=F32
            )
            out = (out * D ** (-0.5)).astype(BF)
            ib[k, 2 * j] = out[:, :128]
            ib[k, 2 * j + 1] = out[:, 128:]
            return carry

        lax.fori_loop(0, RT // 256, part, 0)
        v_far(k, 0).start()
        v_far(k, 1).start()
        v_near(k, 0, 1).start()
        v_near(k, 1, 0).start()
        u_core(k).wait_recv()

        def add(i, carry):
            tb[k, c, i] = (tb[k, c, i].astype(F32) + cr[k, i].astype(F32)).astype(BF)
            return carry

        lax.fori_loop(0, 8, add, 0)
        u_far(k, 0).start()
        u_far(k, 1).start()
        u_near(k, 0, 1).start()
        u_near(k, 1, 0).start()

    def scatter2(k):
        for p in range(2):
            slot = (yp, ym)[p] + 4 * p
            v_far(k, p).wait_recv()
            ib[k, slot] = (ib[k, slot].astype(F32) + yf[k, p].astype(F32)).astype(BF)
            v_near(k, p, p).start()
        for p in range(2):
            slot = (zp, zm)[p] + 4 * p
            u_far(k, p).wait_recv()
            tb[k, c, slot] = (tb[k, c, slot].astype(F32) + zf[k, p].astype(F32)).astype(BF)
            u_near(k, p, p).start()

    def scatter3(k):
        for p in range(2):
            for a in range(2):
                v_near(k, p, a).wait_recv()
        slot = oh * 4 + y
        ib[k, slot] = (
            ib[k, slot].astype(F32) + yn[k, 0, oh].astype(F32) + yn[k, 1, oh].astype(F32)
        ).astype(BF)
        v_last(k).start()
        for p in range(2):
            for a in range(2):
                u_near(k, p, a).wait_recv()
        tb[k, c, w_oth] = (
            tb[k, c, w_oth].astype(F32) + zn[k, 0, ol].astype(F32) + zn[k, 1, ol].astype(F32)
        ).astype(BF)
        u_last(k).start()

    def scatter4(k):
        v_last(k).wait_recv()
        ig_out[k] = (
            (ib[k, s].astype(F32) + xhb[k].astype(F32))
            + (yn[k, 0, xh].astype(F32) + yn[k, 1, xh].astype(F32))
        ).astype(BF)
        u_last(k).wait_recv()
        sum_out[k] = (tb[k, c, w_own].astype(F32) + xlb[k].astype(F32)) + (
            zn[k, 0, xl].astype(F32) + zn[k, 1, xl].astype(F32)
        )

    lax.fori_loop(0, CH, gather0, 0)

    def make_slope(i, carry):
        slot = i % 2
        for copy in stage(i, slot):
            copy.wait()
        lin = prev[slot].astype(F32)
        sig = jax.nn.sigmoid(lin)
        rows = pl.ds(pl.multiple_of(i * STAGE, STAGE), STAGE)
        slope[rows, :] = (cotv[slot].astype(F32) * sig * (1.0 + lin * (1.0 - sig))).astype(BF)

        @pl.when(i + 2 < RT // STAGE)
        def _():
            for copy in stage(i + 2, slot):
                copy.start()

        return carry

    lax.fori_loop(0, RT // STAGE, make_slope, 0)

    def step(t, carry):
        def at(lag, work):
            k = t - lag

            @pl.when((k >= 0) & (k < CH))
            def _():
                work(k)

        at(0, gather1)
        at(1, gather2)
        at(2, gather3)
        at(2, multiply)
        at(3, scatter2)
        at(4, scatter3)
        at(5, scatter4)
        return carry

    lax.fori_loop(0, CH + 5, step, 0)

    def drain(k, carry):
        for i in range(7):
            t_copy(k, s, i, 0, d_xh).wait_send()
            w_copy(k, w_own, i, 0, d_xl).wait_send()
        w_core(k).wait_send()
        u_core(k).wait_send()
        u_last(k).wait_send()
        v_last(k).wait_send()
        for p in range(2):
            u_far(k, p).wait_send()
            v_far(k, p).wait_send()
            for a in range(2):
                u_near(k, p, a).wait_send()
                v_near(k, p, a).wait_send()
        return carry

    lax.fori_loop(0, CH, drain, 0)


def exchange(tokens, preact, cotangent, master):
    any_spec = pl.BlockSpec(memory_space=pl.ANY)
    vmem = pl.BlockSpec(memory_space=pltpu.VMEM)
    dma = pltpu.SemaphoreType.DMA
    return pl.pallas_call(
        kernel,
        out_shape=(
            jax.ShapeDtypeStruct((CH, RB, HID), F32),
            jax.ShapeDtypeStruct((CH, CD, TOK), BF),
        ),
        in_specs=[any_spec] * 4,
        out_specs=(vmem, vmem),
        scratch_shapes=[
            pltpu.VMEM((CH, SEQS, CD, TOK), BF),
            pltpu.VMEM((CH, 2, 8, RB, HID), BF),
            pltpu.VMEM((RT, HID), BF),
            pltpu.VMEM((CH, 2, 8, RB, HID), BF),
            pltpu.VMEM((CH, 8, RB, HID), BF),
            pltpu.VMEM((CH, 2, RB, HID), BF),
            pltpu.VMEM((CH, 2, 2, RB, HID), BF),
            pltpu.VMEM((CH, RB, HID), BF),
            pltpu.VMEM((CH, SEQS, CD, TOK), BF),
            pltpu.VMEM((CH, 2, CD, TOK), BF),
            pltpu.VMEM((CH, 2, 2, CD, TOK), BF),
            pltpu.VMEM((CH, CD, TOK), BF),
            pltpu.VMEM((TOK, D), BF),
            pltpu.VMEM((CH, RB, HID), F32),
            pltpu.VMEM((2, STAGE, HID), BF),
            pltpu.VMEM((2, STAGE, HID), BF),
            dma((2,)),
            dma((2, 2)),
            dma((CH, 8)),
            dma((CH, 8)),
            dma((CH, 8)),
            dma((CH, 8)),
            dma((CH, 8)),
            dma((CH, 8)),
            dma((CH, 8)),
            dma((CH, 8)),
        ],
        compiler_params=pltpu.CompilerParams(
            collective_id=0, has_side_effects=True, vmem_limit_bytes=62 * 2**20
        ),
        cost_estimate=pl.CostEstimate(
            flops=4 * RT * HID * D, bytes_accessed=12 * 2**20, transcendentals=RT * HID
        ),
        name="exchange",
    )(tokens, preact, cotangent, master)


def per_device(tokens, preact, cotangent, master, first_moment, second_moment):
    summed, turned = exchange(tokens, preact, cotangent, master.reshape(CH, RB, HID))
    turned = turned.reshape(CH, 2, 2, 4, RB, TOK)
    input_grad = turned.transpose(5, 2, 3, 1, 0, 4).reshape(TOK, D)
    pseudo = summed.reshape(OWN, HID) * (RT * REGIONS) ** (-0.5)
    new_first = 0.9 * first_moment + 0.1 * pseudo
    new_second = 0.999 * second_moment + 0.001 * pseudo * pseudo
    new_master = master - 0.1 * new_first / (jnp.sqrt(new_second) + 0.001)
    return (new_master, new_first, new_second, input_grad)


def solution(mesh):
    block = P("region", "seq")
    rows = P(("region", "seq"), None)
    return jax.shard_map(
        per_device,
        mesh=mesh,
        in_specs=(rows, block, block, block, block, block),
        out_specs=(block, block, block, rows),
        check_vma=False,
    )
```

```python
import jax
import jax.numpy as jnp
from jax import lax
from jax.experimental import pallas as pl
from jax.experimental.pallas import tpu as pltpu
from jax.sharding import PartitionSpec as P

MESH = pl.DeviceIdType.MESH
BF = jnp.bfloat16
F32 = jnp.float32

D = 3584
REGIONS = 16
SEQS = 8
OWN = D // REGIONS
CH = 7
RB = OWN // CH
CD = D // CH
HALF = CD // 2
TOK = 128
HID = 1280
RT = TOK * SEQS
STAGE = 128
Y_FIRST = (2, 4)

ORDER = (
    ("t_own", 1), ("w_own", 1), ("t_cross", 0), ("t_own", 2), ("w_own", 0), ("t_own", 3), ("t_own", 0),
    ("w_own", 5), ("t_cross", 6), ("w_other", 1), ("slope", -1), ("w_own", 2), ("w_own", 3), ("w_pass1", 1),
    ("t_cross", 1), ("t_own", 4), ("w_pass0", 1), ("w_own", 6), ("t_cross", 3), ("t_other", 0),
    ("w_other", 2), ("w_pass0", 3), ("w_pass0", 5), ("w_pass0", 0), ("t_pass0", 0), ("t_own", 5),
    ("w_other", 0), ("t_pass0", 1), ("t_pass1", 0), ("w_other", 5), ("t_other", 1), ("w_own", 4),
    ("w_pass1", 0), ("t_pass0", 2), ("t_other", 6), ("t_pass1", 4), ("t_other", 3), ("w_other", 3),
    ("t_pass1", 1), ("w_pass1", 3), ("w_other", 6), ("t_pass1", 2), ("t_cross", 5), ("w_pass0", 6),
    ("w_other", 4), ("t_pass0", 4), ("w_share", 1), ("w_pass1", 5), ("term", 0), ("w_pass1", 6),
    ("w_pass0", 4), ("w_share", 3), ("w_pass1", 2), ("t_own", 6), ("part", 1), ("w_pass1", 4),
    ("t_pass0", 3), ("t_other", 5), ("t_far", 4), ("w_pass0", 2), ("term", 1), ("u_first", 0),
    ("w_share", 6), ("t_far", 2), ("w_share", 4), ("t_pass1", 3), ("t_cross", 4), ("w_share", 2),
    ("part", 3), ("u_first", 1), ("u_pass0", 0), ("t_cross", 2), ("t_pass1", 6), ("u_pass0", 1),
    ("part", 2), ("w_share", 0), ("t_pass0", 5), ("term", 4), ("term", 2), ("u_pass1", 1), ("t_pass1", 5),
    ("w_share", 5), ("u_first", 4), ("t_pass0", 6), ("v_pass0", 3), ("v_pass0", 1), ("part", 0),
    ("u_cross", 1), ("part", 4), ("term", 5), ("u_first", 2), ("v_pass1", 1), ("term", 3), ("v_pass1", 3),
    ("u_first", 5), ("v_pass1", 0), ("v_cross", 1), ("u_pass0", 4), ("u_pass0", 2), ("v_pass0", 0),
    ("part", 5), ("u_first", 3), ("part", 6), ("u_cross", 4), ("term", 6), ("u_pass1", 2), ("u_pass1", 4),
    ("v_cross", 0), ("v_pass0", 5), ("u_pass0", 3), ("v_end", 1), ("u_cross", 0), ("u_first", 6),
    ("v_cross", 3), ("v_end", 0), ("u_pass1", 5), ("u_pass0", 5), ("v_pass0", 6), ("u_cross", 2),
    ("u_cross", 3), ("v_first", 4), ("u_pass1", 0), ("v_pass1", 6), ("v_first", 2), ("v_cross", 5),
    ("u_end", 0), ("u_pass0", 6), ("u_cross", 5), ("v_end", 3), ("v_pass1", 5), ("u_pass1", 3),
    ("v_cross", 4), ("v_cross", 6), ("u_cross", 6), ("v_cross", 2), ("u_pass1", 6), ("u_end", 2),
    ("u_end", 3), ("v_end", 6), ("v_end", 4), ("u_end", 5), ("u_end", 1), ("v_end", 5), ("u_end", 4),
    ("u_end", 6), ("v_end", 2),
)


def place(d0):
    owner, rest = divmod(d0, OWN)
    k, i = divmod(rest, RB)
    xl, z, c = owner // 8, owner // 2 % 4, owner % 2
    return k, ((c * 2 + xl) * 4 + z) * RB + i


def rcopy(src, dst, send, recv, dev):
    return pltpu.make_async_remote_copy(
        src_ref=src, dst_ref=dst, send_sem=send, recv_sem=recv, device_id=dev, device_id_type=MESH
    )


def plus(*refs):
    total = refs[0][...].astype(F32)
    for ref in refs[1:]:
        total = total + ref[...].astype(F32)
    return total


def kernel(
    tok, pre, cot, mas, sum_out, ig_out,
    tg, wg, slope, tb, cr, zf, zn, xlb, ib, yf, yn, xhb, tokv, masv, prev, cotv,
    in_sem, st_sem, ts, tr, ws, wr, us, ur, vs, vr,
):
    r = lax.axis_index("region")
    s = lax.axis_index("seq")
    xl, z, c = r // 8, (r // 2) % 4, r % 2
    xh, y = s // 4, s % 4
    ol, oh = 1 - xl, 1 - xh
    zp, zm, zo = (z + 1) % 4, (z + 3) % 4, (z + 2) % 4
    yp, ym, yo = (y + 1) % 4, (y + 3) % 4, (y + 2) % 4

    def rdev(a, b, d):
        return (a * 8 + b * 2 + d, s)

    def sdev(a, b):
        return (r, a * 4 + b)

    d_core = rdev(xl, z, 1 - c)
    d_xl = rdev(ol, z, c)
    d_z = (rdev(xl, zp, c), rdev(xl, zm, c))
    d_xh = sdev(oh, y)
    d_y = (sdev(xh, yp), sdev(xh, ym))

    get_tok = pltpu.make_async_copy(tok, tokv, in_sem.at[0])
    get_mas = pltpu.make_async_copy(mas, masv, in_sem.at[1])
    get_tok.start()
    get_mas.start()

    def stage(i, slot):
        rows = pl.ds(pl.multiple_of(i * STAGE, STAGE), STAGE)
        return (
            pltpu.make_async_copy(pre.at[rows], prev.at[slot], st_sem.at[0, slot]),
            pltpu.make_async_copy(cot.at[rows], cotv.at[slot], st_sem.at[1, slot]),
        )

    for i in range(2):
        for copy in stage(i, i):
            copy.start()

    barrier = pltpu.get_barrier_semaphore()
    for dev in (d_core, d_xl, *d_z, d_xh, *d_y):
        pl.semaphore_signal(barrier, inc=1, device_id=dev, device_id_type=MESH)

    get_tok.wait()
    for j in range(D // 128):
        turned = tokv[:, j * 128:(j + 1) * 128].T
        for m in range(128 // RB):
            k, row = place(j * 128 + m * RB)
            tg[k, s, row:row + RB, :] = turned[m * RB:(m + 1) * RB, :]
    get_mas.wait()

    def cast(k, carry):
        wg[k, c, xl * 4 + z] = masv[k].astype(BF)
        return carry

    lax.fori_loop(0, CH, cast, 0)
    pl.semaphore_wait(barrier, 7)

    def t_copy(k, slot, i, dev):
        return rcopy(tg.at[k, slot], tg.at[k, slot], ts.at[k, i], tr.at[k, i], dev)

    def t_half(k, slot, p):
        part = tg.at[k, slot, pl.ds(p * HALF, HALF)]
        return rcopy(part, part, ts.at[k, 5 + p], tr.at[k, 5 + p], d_y[p])

    def t_wait(k, *ids):
        for i in ids:
            t_copy(k, 0, i, d_xh).wait_recv()

    def t_cross(k):
        t_copy(k, s, 0, d_xh).start()

    def t_own(k):
        t_copy(k, s, 1, d_y[0]).start()
        t_copy(k, s, 3, d_y[1]).start()

    def t_other(k):
        t_wait(k, 0)
        t_copy(k, oh * 4 + y, 2, d_y[0]).start()
        t_copy(k, oh * 4 + y, 4, d_y[1]).start()

    def t_pass0(k):
        t_wait(k, 1)
        if k in Y_FIRST:
            t_half(k, xh * 4 + ym, 0).start()
            t_copy(k, xh * 4 + ym, 2, d_xh).start()
        else:
            t_copy(k, xh * 4 + ym, 5, d_y[0]).start()

    def t_pass1(k):
        if k in Y_FIRST:
            t_wait(k, 3)
            t_half(k, xh * 4 + yp, 1).start()
            t_copy(k, xh * 4 + yp, 4, d_xh).start()
        else:
            t_wait(k, 4)
            t_copy(k, oh * 4 + yp, 6, d_y[1]).start()

    def t_far(k):
        t_half(k, 0, 0).wait_recv()
        t_half(k, 0, 1).wait_recv()
        t_copy(k, xh * 4 + yo, 7, d_xh).start()

    def t_done(k):
        if k in Y_FIRST:
            t_wait(k, 0, 2, 4, 7)
        else:
            t_wait(k, 3, 2, 5, 6)

    def t_sent(k):
        for i in (0, 1, 2, 3, 4):
            t_copy(k, 0, i, d_xh).wait_send()
        if k in Y_FIRST:
            t_half(k, 0, 0).wait_send()
            t_half(k, 0, 1).wait_send()
            t_copy(k, 0, 7, d_xh).wait_send()
        else:
            t_copy(k, 0, 5, d_xh).wait_send()
            t_copy(k, 0, 6, d_xh).wait_send()

    def w_copy(k, slot, i, dev):
        return rcopy(wg.at[k, c, slot], wg.at[k, c, slot], ws.at[k, i], wr.at[k, i], dev)

    def w_core(k, half):
        return rcopy(wg.at[k, half], wg.at[k, half], ws.at[k, 7], wr.at[k, 7], d_core)

    def w_wait(k, *ids):
        for i in ids:
            w_copy(k, 0, i, d_xl).wait_recv()

    def w_own(k):
        w_copy(k, xl * 4 + z, 0, d_xl).start()
        w_copy(k, xl * 4 + z, 1, d_z[0]).start()
        w_copy(k, xl * 4 + z, 3, d_z[1]).start()

    def w_other(k):
        w_wait(k, 0)
        w_copy(k, ol * 4 + z, 2, d_z[0]).start()
        w_copy(k, ol * 4 + z, 4, d_z[1]).start()

    def w_pass0(k):
        w_wait(k, 1)
        w_copy(k, xl * 4 + zm, 5, d_z[0]).start()

    def w_pass1(k):
        w_wait(k, 4)
        w_copy(k, ol * 4 + zp, 6, d_z[1]).start()

    def w_share(k):
        w_wait(k, 3, 2, 5, 6)
        w_core(k, c).start()

    def w_sent(k):
        for i in range(7):
            w_copy(k, 0, i, d_xl).wait_send()
        w_core(k, c).wait_send()

    def u_core(k):
        return rcopy(tb.at[k, 1 - c], cr.at[k], us.at[k, 0], ur.at[k, 0], d_core)

    def u_far(k, p):
        slot = (ol, xl)[p] * 4 + zo
        return rcopy(tb.at[k, c, slot], zf.at[k, p], us.at[k, 1 + p], ur.at[k, 1 + p], d_z[p])

    def u_near(k, p, a):
        slot = ((ol, xl)[a] * 4) + (zp, zm)[p]
        i = 3 + 2 * p + a
        return rcopy(tb.at[k, c, slot], zn.at[k, p, a], us.at[k, i], ur.at[k, i], d_z[p])

    def u_last(k):
        return rcopy(tb.at[k, c, ol * 4 + z], xlb.at[k], us.at[k, 7], ur.at[k, 7], d_xl)

    def term(k):
        t_done(k)

        def tile(j, carry):
            cols = pl.ds(pl.multiple_of(j * 256, 256), 256)
            left = jnp.concatenate([tg[k, i] for i in range(SEQS)], axis=1)
            out = jnp.dot(left, slope[:, cols], preferred_element_type=F32)
            tb[k, :, :, :, cols] = out.astype(BF).reshape(2, 8, RB, 256)
            return carry

        lax.fori_loop(0, HID // 256, tile, 0)
        u_core(k).start()

    def u_first(k):
        u_core(k).wait_recv()

        def add(i, carry):
            tb[k, c, i] = plus(tb.at[k, c, i], cr.at[k, i]).astype(BF)
            return carry

        lax.fori_loop(0, 8, add, 0)
        u_far(k, 0).start()
        u_far(k, 1).start()
        u_near(k, 0, 1).start()
        u_near(k, 1, 0).start()

    def u_pass(k, p):
        slot = (ol, xl)[p] * 4 + (zp, zm)[p]
        u_far(k, p).wait_recv()
        tb[k, c, slot] = plus(tb.at[k, c, slot], zf.at[k, p]).astype(BF)
        u_near(k, p, p).start()

    def u_cross(k):
        u_near(k, 0, 0).wait_recv()
        u_near(k, 1, 0).wait_recv()
        slot = ol * 4 + z
        tb[k, c, slot] = plus(tb.at[k, c, slot], zn.at[k, 0, 0], zn.at[k, 1, 0]).astype(BF)
        u_last(k).start()

    def u_end(k):
        u_near(k, 0, 1).wait_recv()
        u_near(k, 1, 1).wait_recv()
        u_last(k).wait_recv()
        sum_out[k] = plus(tb.at[k, c, xl * 4 + z], xlb.at[k], zn.at[k, 0, 1], zn.at[k, 1, 1])
        u_core(k).wait_send()
        u_last(k).wait_send()
        for p in range(2):
            u_far(k, p).wait_send()
            u_near(k, p, 0).wait_send()
            u_near(k, p, 1).wait_send()
        w_sent(k)

    def v_far(k, p):
        slot = (oh, xh)[p] * 4 + yo
        return rcopy(ib.at[k, slot], yf.at[k, p], vs.at[k, 1 + p], vr.at[k, 1 + p], d_y[p])

    def v_near(k, p, a):
        slot = (oh, xh)[a] * 4 + (yp, ym)[p]
        i = 3 + 2 * p + a
        return rcopy(ib.at[k, slot], yn.at[k, 2 * p + a], vs.at[k, i], vr.at[k, i], d_y[p])

    def v_last(k):
        return rcopy(ib.at[k, oh * 4 + y], xhb.at[k], vs.at[k, 7], vr.at[k, 7], d_xh)

    def v_four(k):
        return rcopy(ib.at[k, pl.ds(oh * 4, 4)], yn.at[k], vs.at[k, 0], vr.at[k, 0], d_xh)

    def v_half(k, p):
        rows = pl.ds(p * HALF, HALF)
        src = ib.at[k, xh * 4 + yo, rows]
        return rcopy(src, xhb.at[k, rows], vs.at[k, 1 + p], vr.at[k, 1 + p], d_y[p])

    def v_side(k, p, a):
        rows = pl.ds(a * HALF, HALF)
        i = 3 + 2 * p + a
        src = ib.at[k, xh * 4 + (yp, ym)[p], rows]
        return rcopy(src, yf.at[k, p, rows], vs.at[k, i], vr.at[k, i], d_y[p])

    def part(k):
        w_core(k, 1 - c).wait_recv()

        def tile(j, carry):
            rows = pl.ds(pl.multiple_of(j * 256, 256), 256)
            left = wg[k].reshape(CD, HID)
            out = lax.dot_general(
                left, slope[rows, :], (((1,), (1,)), ((), ())), preferred_element_type=F32
            )
            out = (out * D ** (-0.5)).astype(BF)
            ib[k, 2 * j] = out[:, :128]
            ib[k, 2 * j + 1] = out[:, 128:]
            return carry

        lax.fori_loop(0, RT // 256, tile, 0)
        if k in Y_FIRST:
            v_four(k).start()
        else:
            v_far(k, 0).start()
            v_far(k, 1).start()
            v_near(k, 0, 1).start()
            v_near(k, 1, 0).start()

    def v_pass(k, p):
        slot = (oh, xh)[p] * 4 + (yp, ym)[p]
        v_far(k, p).wait_recv()
        ib[k, slot] = plus(ib.at[k, slot], yf.at[k, p]).astype(BF)
        v_near(k, p, p).start()

    def v_first(k):
        v_four(k).wait_recv()

        def add(i, carry):
            ib[k, xh * 4 + i] = plus(ib.at[k, xh * 4 + i], yn.at[k, i]).astype(BF)
            return carry

        lax.fori_loop(0, 4, add, 0)
        v_half(k, 0).start()
        v_half(k, 1).start()
        v_side(k, 0, 1).start()
        v_side(k, 1, 0).start()

    def v_cross(k):
        if k in Y_FIRST:
            for p in range(2):
                rows = pl.ds(p * HALF, HALF)
                slot = xh * 4 + (yp, ym)[p]
                v_half(k, p).wait_recv()
                ib[k, slot, rows] = plus(ib.at[k, slot, rows], xhb.at[k, rows]).astype(BF)
                v_side(k, p, p).start()
        else:
            v_near(k, 0, 0).wait_recv()
            v_near(k, 1, 0).wait_recv()
            slot = oh * 4 + y
            ib[k, slot] = plus(ib.at[k, slot], yn.at[k, 0], yn.at[k, 2]).astype(BF)
            v_last(k).start()

    def v_end(k):
        if k in Y_FIRST:
            for p in range(2):
                v_side(k, p, 0).wait_recv()
                v_side(k, p, 1).wait_recv()
            ig_out[k] = plus(ib.at[k, s], yf.at[k, 0], yf.at[k, 1]).astype(BF)
            v_four(k).wait_send()
            for p in range(2):
                v_half(k, p).wait_send()
                v_side(k, p, 0).wait_send()
                v_side(k, p, 1).wait_send()
        else:
            v_near(k, 0, 1).wait_recv()
            v_near(k, 1, 1).wait_recv()
            v_last(k).wait_recv()
            ig_out[k] = plus(ib.at[k, s], xhb.at[k], yn.at[k, 1], yn.at[k, 3]).astype(BF)
            v_last(k).wait_send()
            for p in range(2):
                v_far(k, p).wait_send()
                v_near(k, p, 0).wait_send()
                v_near(k, p, 1).wait_send()
        t_sent(k)

    def make_slope(i, carry):
        slot = i % 2
        for copy in stage(i, slot):
            copy.wait()
        lin = prev[slot].astype(F32)
        sig = jax.nn.sigmoid(lin)
        rows = pl.ds(pl.multiple_of(i * STAGE, STAGE), STAGE)
        slope[rows, :] = (cotv[slot].astype(F32) * sig * (1.0 + lin * (1.0 - sig))).astype(BF)

        @pl.when(i + 2 < RT // STAGE)
        def _():
            for copy in stage(i + 2, slot):
                copy.start()

        return carry

    work = dict(
        t_cross=t_cross, t_own=t_own, t_other=t_other, t_pass0=t_pass0, t_pass1=t_pass1, t_far=t_far,
        w_own=w_own, w_other=w_other, w_pass0=w_pass0, w_pass1=w_pass1, w_share=w_share,
        term=term, u_first=u_first, u_cross=u_cross, u_end=u_end,
        u_pass0=lambda k: u_pass(k, 0), u_pass1=lambda k: u_pass(k, 1),
        part=part, v_first=v_first, v_cross=v_cross, v_end=v_end,
        v_pass0=lambda k: v_pass(k, 0), v_pass1=lambda k: v_pass(k, 1),
        slope=lambda k: lax.fori_loop(0, RT // STAGE, make_slope, 0),
    )
    for name, k in ORDER:
        work[name](k)


def exchange(tokens, preact, cotangent, master):
    any_spec = pl.BlockSpec(memory_space=pl.ANY)
    vmem = pl.BlockSpec(memory_space=pltpu.VMEM)
    dma = pltpu.SemaphoreType.DMA
    return pl.pallas_call(
        kernel,
        out_shape=(
            jax.ShapeDtypeStruct((CH, RB, HID), F32),
            jax.ShapeDtypeStruct((CH, CD, TOK), BF),
        ),
        in_specs=[any_spec] * 4,
        out_specs=(vmem, vmem),
        scratch_shapes=[
            pltpu.VMEM((CH, SEQS, CD, TOK), BF),
            pltpu.VMEM((CH, 2, 8, RB, HID), BF),
            pltpu.VMEM((RT, HID), BF),
            pltpu.VMEM((CH, 2, 8, RB, HID), BF),
            pltpu.VMEM((CH, 8, RB, HID), BF),
            pltpu.VMEM((CH, 2, RB, HID), BF),
            pltpu.VMEM((CH, 2, 2, RB, HID), BF),
            pltpu.VMEM((CH, RB, HID), BF),
            pltpu.VMEM((CH, SEQS, CD, TOK), BF),
            pltpu.VMEM((CH, 2, CD, TOK), BF),
            pltpu.VMEM((CH, 4, CD, TOK), BF),
            pltpu.VMEM((CH, CD, TOK), BF),
            pltpu.VMEM((TOK, D), BF),
            pltpu.VMEM((CH, RB, HID), F32),
            pltpu.VMEM((2, STAGE, HID), BF),
            pltpu.VMEM((2, STAGE, HID), BF),
            dma((2,)),
            dma((2, 2)),
            *[dma((CH, 8)) for _ in range(8)],
        ],
        compiler_params=pltpu.CompilerParams(
            collective_id=0, has_side_effects=True, vmem_limit_bytes=62 * 2**20
        ),
        cost_estimate=pl.CostEstimate(
            flops=4 * RT * HID * D, bytes_accessed=12 * 2**20, transcendentals=RT * HID
        ),
        name="exchange",
    )(tokens, preact, cotangent, master)


def per_device(tokens, preact, cotangent, master, first_moment, second_moment):
    summed, turned = exchange(tokens, preact, cotangent, master.reshape(CH, RB, HID))
    turned = turned.reshape(CH, 2, 2, 4, RB, TOK)
    input_grad = turned.transpose(5, 2, 3, 1, 0, 4).reshape(TOK, D)
    pseudo = summed.reshape(OWN, HID) * (RT * REGIONS) ** (-0.5)
    new_first = 0.9 * first_moment + 0.1 * pseudo
    new_second = 0.999 * second_moment + 0.001 * pseudo * pseudo
    new_master = master - 0.1 * new_first / (jnp.sqrt(new_second) + 0.001)
    return (new_master, new_first, new_second, input_grad)


def solution(mesh):
    block = P("region", "seq")
    rows = P(("region", "seq"), None)
    return jax.shard_map(
        per_device,
        mesh=mesh,
        in_specs=(rows, block, block, block, block, block),
        out_specs=(block, block, block, rows),
        check_vma=False,
    )
```

```python
import jax
import jax.numpy as jnp
from jax import lax
from jax.experimental import pallas as pl
from jax.experimental.pallas import tpu as pltpu
from jax.sharding import PartitionSpec as P

MESH = pl.DeviceIdType.MESH
BF = jnp.bfloat16
F32 = jnp.float32

D = 3584
REGIONS = 16
SEQS = 8
OWN = D // REGIONS
CH = 7
RB = OWN // CH
CD = D // CH
HALF = CD // 2
TOK = 128
HID = 1280
RT = TOK * SEQS
STAGE = 128
Y_FIRST = (2, 4)

ORDER = (
    ("t_own", 1), ("w_own", 1), ("t_cross", 0), ("t_own", 2), ("w_own", 0), ("t_own", 3), ("t_own", 0),
    ("w_own", 5), ("t_cross", 6), ("w_other", 1), ("slope", -1), ("w_own", 2), ("w_own", 3), ("w_pass1", 1),
    ("t_cross", 1), ("t_own", 4), ("w_pass0", 1), ("w_own", 6), ("t_cross", 3), ("t_other", 0),
    ("w_other", 2), ("w_pass0", 3), ("w_pass0", 5), ("w_pass0", 0), ("t_pass0", 0), ("t_own", 5),
    ("w_other", 0), ("t_pass0", 1), ("t_pass1", 0), ("w_other", 5), ("t_other", 1), ("w_own", 4),
    ("w_pass1", 0), ("t_pass0", 2), ("t_other", 6), ("t_pass1", 4), ("t_other", 3), ("w_other", 3),
    ("t_pass1", 1), ("w_pass1", 3), ("w_other", 6), ("t_pass1", 2), ("t_cross", 5), ("w_pass0", 6),
    ("w_other", 4), ("t_pass0", 4), ("w_share", 1), ("w_pass1", 5), ("term", 0), ("w_pass1", 6),
    ("w_pass0", 4), ("w_share", 3), ("w_pass1", 2), ("t_own", 6), ("part", 1), ("w_pass1", 4),
    ("t_pass0", 3), ("t_other", 5), ("t_far", 4), ("w_pass0", 2), ("term", 1), ("u_first", 0),
    ("w_share", 6), ("t_far", 2), ("w_share", 4), ("t_pass1", 3), ("t_cross", 4), ("w_share", 2),
    ("part", 3), ("u_first", 1), ("u_pass0", 0), ("t_cross", 2), ("t_pass1", 6), ("u_pass0", 1),
    ("part", 2), ("w_share", 0), ("t_pass0", 5), ("term", 4), ("term", 2), ("u_pass1", 1), ("t_pass1", 5),
    ("w_share", 5), ("u_first", 4), ("t_pass0", 6), ("v_pass0", 3), ("v_pass0", 1), ("part", 0),
    ("u_cross", 1), ("part", 4), ("term", 5), ("u_first", 2), ("v_pass1", 1), ("term", 3), ("v_pass1", 3),
    ("u_first", 5), ("v_pass1", 0), ("v_cross", 1), ("u_pass0", 4), ("u_pass0", 2), ("v_pass0", 0),
    ("part", 5), ("u_first", 3), ("part", 6), ("u_cross", 4), ("term", 6), ("u_pass1", 2), ("u_pass1", 4),
    ("v_cross", 0), ("v_pass0", 5), ("u_pass0", 3), ("v_end", 1), ("u_cross", 0), ("u_first", 6),
    ("v_cross", 3), ("v_end", 0), ("u_pass1", 5), ("u_pass0", 5), ("v_pass0", 6), ("u_cross", 2),
    ("u_cross", 3), ("v_first", 4), ("u_pass1", 0), ("v_pass1", 6), ("v_first", 2), ("v_cross", 5),
    ("u_end", 0), ("u_pass0", 6), ("u_cross", 5), ("v_end", 3), ("v_pass1", 5), ("u_pass1", 3),
    ("v_cross", 4), ("v_cross", 6), ("u_cross", 6), ("v_cross", 2), ("u_pass1", 6), ("u_end", 2),
    ("u_end", 3), ("v_end", 6), ("v_end", 4), ("u_end", 5), ("u_end", 1), ("v_end", 5), ("u_end", 4),
    ("u_end", 6), ("v_end", 2),
)


def place(d0):
    owner, rest = divmod(d0, OWN)
    k, i = divmod(rest, RB)
    xl, z, c = owner // 8, owner // 2 % 4, owner % 2
    return k, ((c * 2 + xl) * 4 + z) * RB + i


def rcopy(src, dst, send, recv, dev):
    return pltpu.make_async_remote_copy(
        src_ref=src, dst_ref=dst, send_sem=send, recv_sem=recv, device_id=dev, device_id_type=MESH
    )


def plus(*refs):
    total = refs[0][...].astype(F32)
    for ref in refs[1:]:
        total = total + ref[...].astype(F32)
    return total


def kernel(
    tok, pre, cot, mas, sum_out, ig_out,
    tg, wg, slope, tb, cr, zf, zn, xlb, ib, yf, yn, xhb, tokv, masv, prev, cotv,
    in_sem, st_sem, ts, tr, ws, wr, us, ur, vs, vr,
):
    r = lax.axis_index("region")
    s = lax.axis_index("seq")
    xl, z, c = r // 8, (r // 2) % 4, r % 2
    xh, y = s // 4, s % 4
    ol, oh = 1 - xl, 1 - xh
    zp, zm, zo = (z + 1) % 4, (z + 3) % 4, (z + 2) % 4
    yp, ym, yo = (y + 1) % 4, (y + 3) % 4, (y + 2) % 4

    def rdev(a, b, d):
        return (a * 8 + b * 2 + d, s)

    def sdev(a, b):
        return (r, a * 4 + b)

    d_core = rdev(xl, z, 1 - c)
    d_xl = rdev(ol, z, c)
    d_z = (rdev(xl, zp, c), rdev(xl, zm, c))
    d_xh = sdev(oh, y)
    d_y = (sdev(xh, yp), sdev(xh, ym))

    get_tok = pltpu.make_async_copy(tok, tokv, in_sem.at[0])
    get_mas = pltpu.make_async_copy(mas, masv, in_sem.at[1])
    get_tok.start()
    get_mas.start()

    def stage(i, slot):
        rows = pl.ds(pl.multiple_of(i * STAGE, STAGE), STAGE)
        return (
            pltpu.make_async_copy(pre.at[rows], prev.at[slot], st_sem.at[0, slot]),
            pltpu.make_async_copy(cot.at[rows], cotv.at[slot], st_sem.at[1, slot]),
        )

    for i in range(2):
        for copy in stage(i, i):
            copy.start()

    barrier = pltpu.get_barrier_semaphore()
    for dev in (d_core, d_xl, *d_z, d_xh, *d_y):
        pl.semaphore_signal(barrier, inc=1, device_id=dev, device_id_type=MESH)

    get_tok.wait()
    for j in range(D // 128):
        turned = tokv[:, j * 128:(j + 1) * 128].T
        for m in range(128 // RB):
            k, row = place(j * 128 + m * RB)
            tg[k, s, row:row + RB, :] = turned[m * RB:(m + 1) * RB, :]
    get_mas.wait()

    def cast(k, carry):
        wg[k, c, xl * 4 + z] = masv[k].astype(BF)
        return carry

    lax.fori_loop(0, CH, cast, 0)
    pl.semaphore_wait(barrier, 7)

    def t_copy(k, slot, i, dev):
        return rcopy(tg.at[k, slot], tg.at[k, slot], ts.at[k, i], tr.at[k, i], dev)

    def t_half(k, slot, p):
        part = tg.at[k, slot, pl.ds(p * HALF, HALF)]
        return rcopy(part, part, ts.at[k, 5 + p], tr.at[k, 5 + p], d_y[p])

    def t_wait(k, *ids):
        for i in ids:
            t_copy(k, 0, i, d_xh).wait_recv()

    def t_cross(k):
        t_copy(k, s, 0, d_xh).start()

    def t_own(k):
        t_copy(k, s, 1, d_y[0]).start()
        t_copy(k, s, 3, d_y[1]).start()

    def t_other(k):
        t_wait(k, 0)
        t_copy(k, oh * 4 + y, 2, d_y[0]).start()
        t_copy(k, oh * 4 + y, 4, d_y[1]).start()

    def t_pass0(k):
        t_wait(k, 1)
        if k in Y_FIRST:
            t_half(k, xh * 4 + ym, 0).start()
            t_copy(k, xh * 4 + ym, 2, d_xh).start()
        else:
            t_copy(k, xh * 4 + ym, 5, d_y[0]).start()

    def t_pass1(k):
        if k in Y_FIRST:
            t_wait(k, 3)
            t_half(k, xh * 4 + yp, 1).start()
            t_copy(k, xh * 4 + yp, 4, d_xh).start()
        else:
            t_wait(k, 4)
            t_copy(k, oh * 4 + yp, 6, d_y[1]).start()

    def t_far(k):
        t_half(k, 0, 0).wait_recv()
        t_half(k, 0, 1).wait_recv()
        t_copy(k, xh * 4 + yo, 7, d_xh).start()

    def t_done(k):
        if k in Y_FIRST:
            t_wait(k, 0, 2, 4, 7)
        else:
            t_wait(k, 3, 2, 5, 6)

    def t_sent(k):
        for i in (0, 1, 2, 3, 4):
            t_copy(k, 0, i, d_xh).wait_send()
        if k in Y_FIRST:
            t_half(k, 0, 0).wait_send()
            t_half(k, 0, 1).wait_send()
            t_copy(k, 0, 7, d_xh).wait_send()
        else:
            t_copy(k, 0, 5, d_xh).wait_send()
            t_copy(k, 0, 6, d_xh).wait_send()

    def w_copy(k, slot, i, dev):
        return rcopy(wg.at[k, c, slot], wg.at[k, c, slot], ws.at[k, i], wr.at[k, i], dev)

    def w_core(k, half):
        return rcopy(wg.at[k, half], wg.at[k, half], ws.at[k, 7], wr.at[k, 7], d_core)

    def w_wait(k, *ids):
        for i in ids:
            w_copy(k, 0, i, d_xl).wait_recv()

    def w_own(k):
        w_copy(k, xl * 4 + z, 0, d_xl).start()
        w_copy(k, xl * 4 + z, 1, d_z[0]).start()
        w_copy(k, xl * 4 + z, 3, d_z[1]).start()

    def w_other(k):
        w_wait(k, 0)
        w_copy(k, ol * 4 + z, 2, d_z[0]).start()
        w_copy(k, ol * 4 + z, 4, d_z[1]).start()

    def w_pass0(k):
        w_wait(k, 1)
        w_copy(k, xl * 4 + zm, 5, d_z[0]).start()

    def w_pass1(k):
        w_wait(k, 4)
        w_copy(k, ol * 4 + zp, 6, d_z[1]).start()

    def w_share(k):
        w_wait(k, 3, 2, 5, 6)
        w_core(k, c).start()

    def w_sent(k):
        for i in range(7):
            w_copy(k, 0, i, d_xl).wait_send()
        w_core(k, c).wait_send()

    def u_core(k):
        return rcopy(tb.at[k, 1 - c], cr.at[k], us.at[k, 0], ur.at[k, 0], d_core)

    def u_far(k, p):
        slot = (ol, xl)[p] * 4 + zo
        return rcopy(tb.at[k, c, slot], zf.at[k, p], us.at[k, 1 + p], ur.at[k, 1 + p], d_z[p])

    def u_near(k, p, a):
        slot = ((ol, xl)[a] * 4) + (zp, zm)[p]
        i = 3 + 2 * p + a
        return rcopy(tb.at[k, c, slot], zn.at[k, p, a], us.at[k, i], ur.at[k, i], d_z[p])

    def u_last(k):
        return rcopy(tb.at[k, c, ol * 4 + z], xlb.at[k], us.at[k, 7], ur.at[k, 7], d_xl)

    def term(k):
        t_done(k)

        def tile(j, carry):
            cols = pl.ds(pl.multiple_of(j * 256, 256), 256)
            left = jnp.concatenate([tg[k, i] for i in range(SEQS)], axis=1)
            out = jnp.dot(left, slope[:, cols], preferred_element_type=F32)
            tb[k, :, :, :, cols] = out.astype(BF).reshape(2, 8, RB, 256)
            return carry

        lax.fori_loop(0, HID // 256, tile, 0)
        u_core(k).start()

    def u_first(k):
        u_core(k).wait_recv()

        def add(i, carry):
            tb[k, c, i] = plus(tb.at[k, c, i], cr.at[k, i]).astype(BF)
            return carry

        lax.fori_loop(0, 8, add, 0)
        u_far(k, 0).start()
        u_far(k, 1).start()
        u_near(k, 0, 1).start()
        u_near(k, 1, 0).start()

    def u_pass(k, p):
        slot = (ol, xl)[p] * 4 + (zp, zm)[p]
        u_far(k, p).wait_recv()
        tb[k, c, slot] = plus(tb.at[k, c, slot], zf.at[k, p]).astype(BF)
        u_near(k, p, p).start()

    def u_cross(k):
        u_near(k, 0, 0).wait_recv()
        u_near(k, 1, 0).wait_recv()
        slot = ol * 4 + z
        tb[k, c, slot] = plus(tb.at[k, c, slot], zn.at[k, 0, 0], zn.at[k, 1, 0]).astype(BF)
        u_last(k).start()

    def u_end(k):
        u_near(k, 0, 1).wait_recv()
        u_near(k, 1, 1).wait_recv()
        u_last(k).wait_recv()
        sum_out[k] = plus(tb.at[k, c, xl * 4 + z], xlb.at[k], zn.at[k, 0, 1], zn.at[k, 1, 1])
        u_core(k).wait_send()
        u_last(k).wait_send()
        for p in range(2):
            u_far(k, p).wait_send()
            u_near(k, p, 0).wait_send()
            u_near(k, p, 1).wait_send()
        w_sent(k)

    def v_far(k, p):
        slot = (oh, xh)[p] * 4 + yo
        return rcopy(ib.at[k, slot], yf.at[k, p], vs.at[k, 1 + p], vr.at[k, 1 + p], d_y[p])

    def v_near(k, p, a):
        slot = (oh, xh)[a] * 4 + (yp, ym)[p]
        i = 3 + 2 * p + a
        return rcopy(ib.at[k, slot], yn.at[k, 2 * p + a], vs.at[k, i], vr.at[k, i], d_y[p])

    def v_last(k):
        return rcopy(ib.at[k, oh * 4 + y], xhb.at[k], vs.at[k, 7], vr.at[k, 7], d_xh)

    def v_four(k):
        return rcopy(ib.at[k, pl.ds(oh * 4, 4)], yn.at[k], vs.at[k, 0], vr.at[k, 0], d_xh)

    def v_half(k, p):
        rows = pl.ds(p * HALF, HALF)
        src = ib.at[k, xh * 4 + yo, rows]
        return rcopy(src, xhb.at[k, rows], vs.at[k, 1 + p], vr.at[k, 1 + p], d_y[p])

    def v_side(k, p, a):
        rows = pl.ds(a * HALF, HALF)
        i = 3 + 2 * p + a
        src = ib.at[k, xh * 4 + (yp, ym)[p], rows]
        return rcopy(src, yf.at[k, p, rows], vs.at[k, i], vr.at[k, i], d_y[p])

    def part(k):
        w_core(k, 1 - c).wait_recv()

        def tile(j, carry):
            rows = pl.ds(pl.multiple_of(j * 256, 256), 256)
            left = wg[k].reshape(CD, HID)
            out = lax.dot_general(
                left, slope[rows, :], (((1,), (1,)), ((), ())), preferred_element_type=F32
            )
            out = (out * D ** (-0.5)).astype(BF)
            ib[k, 2 * j] = out[:, :128]
            ib[k, 2 * j + 1] = out[:, 128:]
            return carry

        lax.fori_loop(0, RT // 256, tile, 0)
        if k in Y_FIRST:
            v_four(k).start()
        else:
            v_far(k, 0).start()
            v_far(k, 1).start()
            v_near(k, 0, 1).start()
            v_near(k, 1, 0).start()

    def v_pass(k, p):
        slot = (oh, xh)[p] * 4 + (yp, ym)[p]
        v_far(k, p).wait_recv()
        ib[k, slot] = plus(ib.at[k, slot], yf.at[k, p]).astype(BF)
        v_near(k, p, p).start()

    def v_first(k):
        v_four(k).wait_recv()

        def add(i, carry):
            ib[k, xh * 4 + i] = plus(ib.at[k, xh * 4 + i], yn.at[k, i]).astype(BF)
            return carry

        lax.fori_loop(0, 4, add, 0)
        v_half(k, 0).start()
        v_half(k, 1).start()
        v_side(k, 0, 1).start()
        v_side(k, 1, 0).start()

    def v_cross(k):
        if k in Y_FIRST:
            for p in range(2):
                rows = pl.ds(p * HALF, HALF)
                slot = xh * 4 + (yp, ym)[p]
                v_half(k, p).wait_recv()
                ib[k, slot, rows] = plus(ib.at[k, slot, rows], xhb.at[k, rows]).astype(BF)
                v_side(k, p, p).start()
        else:
            v_near(k, 0, 0).wait_recv()
            v_near(k, 1, 0).wait_recv()
            slot = oh * 4 + y
            ib[k, slot] = plus(ib.at[k, slot], yn.at[k, 0], yn.at[k, 2]).astype(BF)
            v_last(k).start()

    def v_end(k):
        if k in Y_FIRST:
            for p in range(2):
                v_side(k, p, 0).wait_recv()
                v_side(k, p, 1).wait_recv()
            ig_out[k] = plus(ib.at[k, s], yf.at[k, 0], yf.at[k, 1]).astype(BF)
            v_four(k).wait_send()
            for p in range(2):
                v_half(k, p).wait_send()
                v_side(k, p, 0).wait_send()
                v_side(k, p, 1).wait_send()
        else:
            v_near(k, 0, 1).wait_recv()
            v_near(k, 1, 1).wait_recv()
            v_last(k).wait_recv()
            ig_out[k] = plus(ib.at[k, s], xhb.at[k], yn.at[k, 1], yn.at[k, 3]).astype(BF)
            v_last(k).wait_send()
            for p in range(2):
                v_far(k, p).wait_send()
                v_near(k, p, 0).wait_send()
                v_near(k, p, 1).wait_send()
        t_sent(k)

    def make_slope(i, carry):
        slot = i % 2
        for copy in stage(i, slot):
            copy.wait()
        lin = prev[slot].astype(F32)
        sig = jax.nn.sigmoid(lin)
        rows = pl.ds(pl.multiple_of(i * STAGE, STAGE), STAGE)
        slope[rows, :] = (cotv[slot].astype(F32) * sig * (1.0 + lin * (1.0 - sig))).astype(BF)

        @pl.when(i + 2 < RT // STAGE)
        def _():
            for copy in stage(i + 2, slot):
                copy.start()

        return carry

    work = dict(
        t_cross=t_cross, t_own=t_own, t_other=t_other, t_pass0=t_pass0, t_pass1=t_pass1, t_far=t_far,
        w_own=w_own, w_other=w_other, w_pass0=w_pass0, w_pass1=w_pass1, w_share=w_share,
        term=term, u_first=u_first, u_cross=u_cross, u_end=u_end,
        u_pass0=lambda k: u_pass(k, 0), u_pass1=lambda k: u_pass(k, 1),
        part=part, v_first=v_first, v_cross=v_cross, v_end=v_end,
        v_pass0=lambda k: v_pass(k, 0), v_pass1=lambda k: v_pass(k, 1),
        slope=lambda k: lax.fori_loop(0, RT // STAGE, make_slope, 0),
    )
    for name, k in ORDER:
        work[name](k)


def exchange(tokens, preact, cotangent, master):
    any_spec = pl.BlockSpec(memory_space=pl.ANY)
    dma = pltpu.SemaphoreType.DMA
    return pl.pallas_call(
        kernel,
        out_shape=(
            pltpu.VMEM((CH, RB, HID), F32),
            pltpu.VMEM((CH, CD, TOK), BF),
        ),
        in_specs=[any_spec] * 4,
        out_specs=(pl.BlockSpec(memory_space=pltpu.VMEM),) * 2,
        scratch_shapes=[
            pltpu.VMEM((CH, SEQS, CD, TOK), BF),
            pltpu.VMEM((CH, 2, 8, RB, HID), BF),
            pltpu.VMEM((RT, HID), BF),
            pltpu.VMEM((CH, 2, 8, RB, HID), BF),
            pltpu.VMEM((CH, 8, RB, HID), BF),
            pltpu.VMEM((CH, 2, RB, HID), BF),
            pltpu.VMEM((CH, 2, 2, RB, HID), BF),
            pltpu.VMEM((CH, RB, HID), BF),
            pltpu.VMEM((CH, SEQS, CD, TOK), BF),
            pltpu.VMEM((CH, 2, CD, TOK), BF),
            pltpu.VMEM((CH, 4, CD, TOK), BF),
            pltpu.VMEM((CH, CD, TOK), BF),
            pltpu.VMEM((TOK, D), BF),
            pltpu.VMEM((CH, RB, HID), F32),
            pltpu.VMEM((2, STAGE, HID), BF),
            pltpu.VMEM((2, STAGE, HID), BF),
            dma((2,)),
            dma((2, 2)),
            *[dma((CH, 8)) for _ in range(8)],
        ],
        compiler_params=pltpu.CompilerParams(
            collective_id=0, has_side_effects=True, vmem_limit_bytes=56 * 2**20
        ),
        cost_estimate=pl.CostEstimate(
            flops=4 * RT * HID * D, bytes_accessed=12 * 2**20, transcendentals=RT * HID
        ),
        name="exchange",
    )(tokens, preact, cotangent, master)


def finish_kernel(
    summed, turned, mas, first, second, new_mas, new_first, new_second, grad,
    insv, outv, gradv, in_sem, out_sem, grad_sem,
):
    def rows(k):
        return pl.ds(k * RB, RB)

    def get(k):
        srcs = (mas.at[rows(k)], first.at[rows(k)], second.at[rows(k)])
        return [pltpu.make_async_copy(src, insv.at[i, k], in_sem.at[i, k]) for i, src in enumerate(srcs)]

    def put(k):
        dsts = (new_mas, new_first, new_second)
        return [
            pltpu.make_async_copy(outv.at[i, k], dst.at[rows(k)], out_sem.at[i, k]) for i, dst in enumerate(dsts)
        ]

    put_grad = pltpu.make_async_copy(gradv, grad, grad_sem)
    for j in range(D // 128):
        pieces = []
        for m in range(128 // RB):
            q, row = place(j * 128 + m * RB)
            pieces.append(turned[q, row:row + RB, :])
        gradv[:, j * 128:(j + 1) * 128] = jnp.concatenate(pieces, axis=0).T
    put_grad.start()
    for k in range(CH):
        pseudo = summed[k] * (RT * REGIONS) ** (-0.5)
        one = 0.9 * first[rows(k), :] + 0.1 * pseudo
        two = 0.999 * second[rows(k), :] + 0.001 * pseudo * pseudo
        outv[0, k] = mas[rows(k), :] - 0.1 * one / (jnp.sqrt(two) + 0.001)
        outv[1, k] = one
        outv[2, k] = two
        for copy in put(k):
            copy.start()
    put_grad.wait()
    for k in range(CH):
        for copy in put(k):
            copy.wait()


def finish(summed, turned, master, first_moment, second_moment):
    any_spec = pl.BlockSpec(memory_space=pl.ANY)
    state = jax.ShapeDtypeStruct((OWN, HID), F32)
    dma = pltpu.SemaphoreType.DMA
    return pl.pallas_call(
        finish_kernel,
        out_shape=(state, state, state, jax.ShapeDtypeStruct((TOK, D), BF)),
        in_specs=[pl.BlockSpec(memory_space=pltpu.VMEM)] * 5,
        out_specs=(any_spec,) * 4,
        scratch_shapes=[
            pltpu.VMEM((3, CH, RB, HID), F32),
            pltpu.VMEM((3, CH, RB, HID), F32),
            pltpu.VMEM((TOK, D), BF),
            dma((3, CH)),
            dma((3, CH)),
            dma,
        ],
        compiler_params=pltpu.CompilerParams(vmem_limit_bytes=16 * 2**20),
        name="finish",
    )(summed, turned, master, first_moment, second_moment)


def per_device(tokens, preact, cotangent, master, first_moment, second_moment):
    summed, turned = exchange(tokens, preact, cotangent, master.reshape(CH, RB, HID))
    return finish(summed, turned, master, first_moment, second_moment)


def solution(mesh):
    block = P("region", "seq")
    rows = P(("region", "seq"), None)
    return jax.shard_map(
        per_device,
        mesh=mesh,
        in_specs=(rows, block, block, block, block, block),
        out_specs=(block, block, block, rows),
        check_vma=False,
    )
```

```python
import jax
import jax.numpy as jnp
from jax import lax
from jax.experimental import pallas as pl
from jax.experimental.pallas import tpu as pltpu
from jax.sharding import PartitionSpec as P

MESH = pl.DeviceIdType.MESH
BF = jnp.bfloat16
F32 = jnp.float32

D = 3584
REGIONS = 16
SEQS = 8
OWN = D // REGIONS
CH = 7
RB = OWN // CH
CD = D // CH
HALF = CD // 2
TOK = 128
HID = 1280
RT = TOK * SEQS
STAGE = 128
ST = RT // STAGE
HT = RT // 2
X_FIRST = (3, 5)
Z_FIRST = tuple(k for k in range(CH) if k not in X_FIRST)

(
    T_OWN, T_PASS0, T_PASS1, T_SHARE, W_OWN, W_OTHER, W_PASS0, W_PASS1, W_SHARE,
    SLOPE0, SLOPE1, S_CROSS, S_PASS, TERM0, TERM1, U_PASS0, U_PASS1, U_TURN,
    U_XPASS0, U_XPASS1, U_END, PART, V_PASS0, V_PASS1, V_CROSS, V_END,
) = range(26)
ORDER = (
    (W_OWN, 3), (T_OWN, 0), (T_OWN, 1), (W_OWN, 6), (SLOPE0, 0), (T_OWN, 3), (W_OWN, 0), (W_OWN, 4),
    (W_OTHER, 3), (W_OTHER, 6), (T_OWN, 4), (W_OWN, 2), (W_PASS0, 3), (S_CROSS, 0), (W_PASS0, 6),
    (T_OWN, 5), (W_OWN, 1), (S_CROSS, 3), (T_PASS0, 1), (SLOPE1, 0), (T_PASS1, 4), (S_CROSS, 2),
    (W_PASS1, 6), (T_OWN, 2), (W_PASS0, 4), (S_CROSS, 1), (W_OTHER, 4), (T_PASS0, 0), (T_PASS1, 3),
    (W_PASS0, 0), (T_PASS1, 0), (W_OTHER, 0), (T_PASS1, 1), (W_SHARE, 6), (W_PASS1, 4), (T_PASS1, 2),
    (T_PASS0, 4), (W_PASS0, 1), (W_PASS1, 0), (T_PASS0, 5), (W_OTHER, 1), (W_SHARE, 4), (T_PASS0, 2),
    (T_PASS1, 5), (W_OWN, 5), (T_PASS0, 3), (T_SHARE, 4), (PART, 6), (W_PASS1, 3), (T_SHARE, 2),
    (T_SHARE, 5), (W_OTHER, 2), (T_SHARE, 0), (T_SHARE, 1), (TERM0, 4), (PART, 4), (TERM0, 2), (T_SHARE, 3),
    (W_SHARE, 3), (TERM0, 5), (TERM0, 1), (V_PASS0, 6), (V_PASS1, 4), (W_PASS0, 5), (W_SHARE, 0),
    (W_PASS0, 2), (V_PASS0, 4), (T_OWN, 6), (TERM0, 0), (S_PASS, 0), (V_PASS1, 6), (V_CROSS, 6),
    (U_PASS1, 4), (W_PASS1, 2), (PART, 0), (V_CROSS, 4), (W_OTHER, 5), (T_PASS1, 6), (TERM1, 5), (TERM1, 4),
    (PART, 3), (TERM1, 2), (W_SHARE, 2), (U_XPASS0, 5), (W_PASS1, 5), (U_XPASS1, 5), (TERM0, 3),
    (V_PASS0, 0), (W_PASS1, 1), (U_PASS1, 1), (U_PASS0, 4), (TERM1, 3), (V_PASS0, 3), (V_PASS1, 3),
    (U_PASS0, 2), (PART, 2), (TERM1, 1), (W_SHARE, 5), (V_CROSS, 0), (TERM1, 0), (U_PASS1, 2), (T_PASS0, 6),
    (V_PASS1, 0), (U_TURN, 4), (PART, 5), (V_PASS1, 2), (U_PASS0, 1), (W_SHARE, 1), (V_CROSS, 3),
    (U_XPASS1, 4), (U_PASS1, 0), (T_SHARE, 6), (U_XPASS1, 3), (U_PASS0, 0), (U_XPASS0, 3), (U_XPASS0, 4),
    (V_PASS0, 5), (V_PASS0, 2), (TERM0, 6), (U_TURN, 1), (TERM1, 6), (U_TURN, 0), (U_TURN, 2), (V_CROSS, 5),
    (PART, 1), (U_PASS1, 6), (V_CROSS, 2), (U_PASS0, 6), (U_XPASS1, 2), (U_XPASS1, 1), (V_PASS1, 5),
    (U_XPASS1, 0), (U_TURN, 3), (U_TURN, 5), (U_XPASS0, 2), (U_XPASS0, 0), (V_PASS0, 1), (U_XPASS0, 1),
    (U_PASS1, 3), (U_TURN, 6), (V_PASS1, 1), (V_END, 3), (V_END, 2), (V_CROSS, 1), (U_END, 4), (U_PASS0, 5),
    (V_END, 0), (V_END, 4), (U_PASS0, 3), (U_XPASS0, 6), (U_PASS1, 5), (U_END, 2), (U_XPASS1, 6),
    (U_END, 0), (V_END, 6), (V_END, 5), (U_END, 5), (U_END, 3), (U_END, 1), (V_END, 1), (U_END, 6),
)

FIRST0 = next(k for name, k in ORDER if name == TERM0)
FIRST1 = next(k for name, k in ORDER if name == TERM1)


def place(d0):
    owner, rest = divmod(d0, OWN)
    k, i = divmod(rest, RB)
    xl, z, c = owner // 8, owner // 2 % 4, owner % 2
    return k, ((c * 4 + z) * 2 + xl) * RB + i


def rcopy(src, dst, send, recv, dev):
    return pltpu.make_async_remote_copy(
        src_ref=src, dst_ref=dst, send_sem=send, recv_sem=recv, device_id=dev, device_id_type=MESH
    )


def plus(*refs):
    total = refs[0][...].astype(F32)
    for ref in refs[1:]:
        total = total + ref[...].astype(F32)
    return total


def kernel(
    tok, pre, cot, mas, sum_out, ig_out,
    tg, tc, wg, slope, sx, tb, zf, zn, xf, xs, xf4, xs4, zf1, zs1, ib, yf, yn, xhb, tokv, masv, prev, cotv,
    in_sem, st_sem, ts, tr, ws, wr, us, ur, vs, vr, ss, sr,
):
    r = lax.axis_index("region")
    s = lax.axis_index("seq")
    xl, z, c = r // 8, (r // 2) % 4, r % 2
    xh, y = s // 4, s % 4
    ol, oh = 1 - xl, 1 - xh
    zp, zm, zo = (z + 1) % 4, (z + 3) % 4, (z + 2) % 4
    yp, ym, yo = (y + 1) % 4, (y + 3) % 4, (y + 2) % 4

    def device(a, b, d, e, f):
        return (a * 8 + b * 2 + d, e * 4 + f)

    d_core = device(xl, z, 1 - c, xh, y)
    d_x = (device(ol, z, c, xh, y), device(ol, z, c, oh, y))
    d_xh = device(xl, z, c, oh, y)
    d_z = (device(xl, zp, c, xh, y), device(xl, zm, c, xh, y))
    d_y = (device(xl, z, c, xh, yp), device(xl, z, c, xh, ym))

    get_tok = pltpu.make_async_copy(tok, tokv, in_sem.at[0])
    get_mas = pltpu.make_async_copy(mas, masv, in_sem.at[1])
    get_tok.start()
    get_mas.start()

    def stage(i, slot):
        half = oh + (i // 4) * (xh - oh)
        rows = pl.ds(pl.multiple_of((half * 4 + i % 4) * STAGE, STAGE), STAGE)
        return rows, (
            pltpu.make_async_copy(pre.at[rows], prev.at[slot], st_sem.at[0, slot]),
            pltpu.make_async_copy(cot.at[rows], cotv.at[slot], st_sem.at[1, slot]),
        )

    for i in range(2):
        for copy in stage(i, i)[1]:
            copy.start()

    barrier = pltpu.get_barrier_semaphore()
    for dev in (d_core, *d_x, d_xh, *d_z, *d_y):
        pl.semaphore_signal(barrier, inc=1, device_id=dev, device_id_type=MESH)

    get_tok.wait()
    for j in range(D // 128):
        turned = tokv[:, j * 128:(j + 1) * 128].T
        for m in range(128 // RB):
            k, row = place(j * 128 + m * RB)
            half, row = divmod(row, HALF)
            tg[k, y, half, row:row + RB, :] = turned[m * RB:(m + 1) * RB, :]
    pl.semaphore_wait(barrier, 8)

    def t_copy(k, slot, i):
        return rcopy(tg.at[k, slot], tg.at[k, slot], ts.at[k, i], tr.at[k, i], d_y[i])

    def t_half(k, slot, p):
        return rcopy(tg.at[k, slot, p], tg.at[k, slot, p], ts.at[k, 2 + p], tr.at[k, 2 + p], d_y[p])

    def t_core(k):
        return rcopy(tg.at[k, :, 1 - c], tc.at[k], ts.at[k, 4], tr.at[k, 4], d_core)

    def t_own(k):
        t_copy(k, y, 0).start()
        t_copy(k, y, 1).start()

    def t_pass(k, p):
        t_copy(k, y, p).wait_recv()
        t_half(k, (ym, yp)[p], p).start()

    def t_share(k):
        t_half(k, yo, 0).wait_recv()
        t_half(k, yo, 1).wait_recv()
        t_core(k).start()

    def t_sent(k):
        for p in range(2):
            t_copy(k, y, p).wait_send()
            t_half(k, y, p).wait_send()
        t_core(k).wait_send()

    def w_copy(k, slot, i, dev):
        return rcopy(wg.at[k, c, slot], wg.at[k, c, slot], ws.at[k, i], wr.at[k, i], dev)

    def w_core(k, half):
        return rcopy(wg.at[k, half], wg.at[k, half], ws.at[k, 7], wr.at[k, 7], d_core)

    def w_wait(k, *ids):
        for i in ids:
            w_copy(k, 0, i, d_x[0]).wait_recv()

    def w_own(k):
        wg[k, c, z * 2 + xl] = masv[k].astype(BF)
        w_copy(k, z * 2 + xl, 0, d_x[0]).start()
        w_copy(k, z * 2 + xl, 1, d_z[0]).start()
        w_copy(k, z * 2 + xl, 3, d_z[1]).start()

    def w_other(k):
        w_wait(k, 0)
        w_copy(k, z * 2 + ol, 2, d_z[0]).start()
        w_copy(k, z * 2 + ol, 4, d_z[1]).start()

    def w_pass0(k):
        w_wait(k, 1)
        w_copy(k, zm * 2 + xl, 5, d_z[0]).start()

    def w_pass1(k):
        w_wait(k, 4)
        w_copy(k, zp * 2 + ol, 6, d_z[1]).start()

    def w_share(k):
        w_wait(k, 3, 2, 5, 6)
        w_core(k, c).start()

    def w_sent(k):
        for i in range(7):
            w_copy(k, 0, i, d_x[0]).wait_send()
        w_core(k, c).wait_send()

    def make_slope(i, carry):
        slot = i % 2
        rows, copies = stage(i, slot)
        for copy in copies:
            copy.wait()
        lin = prev[slot].astype(F32)
        sig = jax.nn.sigmoid(lin)
        slope[rows, :] = (cotv[slot].astype(F32) * sig * (1.0 + lin * (1.0 - sig))).astype(BF)

        @pl.when(i + 2 < ST)
        def _():
            for copy in stage(i + 2, slot)[1]:
                copy.start()

        return carry

    def own_rows():
        return pl.ds(pl.multiple_of(xh * HT, HT), HT)

    def s_copy(i):
        rows = pl.ds(pl.multiple_of((oh * 4 + i) * STAGE, STAGE), STAGE)
        return rcopy(slope.at[rows], sx.at[0, pl.ds(i * STAGE, STAGE)], ss.at[i], sr.at[i], d_xh)

    def s_core(i):
        src = (slope.at[own_rows()], sx.at[0])[i]
        return rcopy(src, sx.at[1 + i], ss.at[4 + i], sr.at[4 + i], d_core)

    def slope0(k):
        lax.fori_loop(0, ST // 2, make_slope, 0)

    def slope1(k):
        lax.fori_loop(ST // 2, ST, make_slope, 0)
        s_core(0).start()

    def s_cross(i):
        s_copy(i).start()

    def s_pass(k):
        for i in range(4):
            s_copy(i).wait_recv()
        s_core(1).start()

    def s_sent():
        for i in range(4):
            s_copy(i).wait_send()
        s_core(0).wait_send()
        s_core(1).wait_send()

    def u_copy(k, i, src, dst, dev):
        return rcopy(src, dst, us.at[k, i], ur.at[k, i], dev)

    def half_rows(a):
        return pl.ds(a * (RB // 2), RB // 2)

    def u_far(k, p):
        if k in X_FIRST:
            n = X_FIRST.index(k)
            src, dst = tb.at[k, zo, 0, xl, half_rows(p)], zf1.at[n, half_rows(p)]
        else:
            n = Z_FIRST.index(k)
            src, dst = tb.at[k, zo, 1 - p], zf.at[n, p]
        return u_copy(k, p, src, dst, d_z[p])

    def u_near(k, p, a):
        slot = (zp, zm)[p]
        if k in X_FIRST:
            n = X_FIRST.index(k)
            src, dst = tb.at[k, slot, 0, xl, half_rows(a)], zs1.at[n, p, half_rows(a)]
        else:
            n = Z_FIRST.index(k)
            src, dst = tb.at[k, slot, a], zn.at[n, p, a]
        return u_copy(k, 2 + 2 * p + a, src, dst, d_z[p])

    def u_xfar(k, p):
        if k in X_FIRST:
            n = X_FIRST.index(k)
            src, dst = tb.at[k, :, 1, xl, half_rows(p)], xf4.at[n, :, half_rows(p)]
        else:
            n = Z_FIRST.index(k)
            src, dst = tb.at[k, z, 1, xl, half_rows(p)], xf.at[n, half_rows(p)]
        return u_copy(k, 6 + p, src, dst, d_x[p])

    def u_xnear(k, p, a):
        if k in X_FIRST:
            n = X_FIRST.index(k)
            src, dst = tb.at[k, :, p, ol, half_rows(a)], xs4.at[n, p, :, half_rows(a)]
        else:
            n = Z_FIRST.index(k)
            src, dst = tb.at[k, z, p, ol, half_rows(a)], xs.at[n, p, half_rows(a)]
        return u_copy(k, 8 + 2 * p + a, src, dst, d_x[p])

    def term(k, h):
        if h == 0:
            t_core(k).wait_recv()
            if k == FIRST0:
                s_core(0).wait_recv()
        elif k == FIRST1:
            s_core(1).wait_recv()

        def tile(j, carry):
            cols = pl.ds(pl.multiple_of(j * 256, 256), 256)
            mine = jnp.concatenate([tg[k, i, c] for i in range(4)], axis=1)
            theirs = jnp.concatenate([tc[k, i] for i in range(4)], axis=1)
            own = slope[own_rows(), cols] if h == 0 else sx[0, :, cols]
            out = jnp.dot(mine, own, preferred_element_type=F32)
            out = out + jnp.dot(theirs, sx[1 + h, :, cols], preferred_element_type=F32)
            tb[k, :, h, :, :, cols] = out.astype(BF).reshape(4, 2, RB, 256)
            return carry

        lax.fori_loop(0, HID // 256, tile, 0)
        if k in Z_FIRST:
            u_far(k, 1 - h).start()
            u_near(k, h, h).start()
        elif h == 1:
            u_xsend(k)

    def u_xsend(k):
        u_xfar(k, 0).start()
        u_xfar(k, 1).start()
        u_xnear(k, 0, 0).start()
        u_xnear(k, 1, 1).start()

    def u_pass(k, p):
        u_far(k, p).wait_recv()
        slot = (zp, zm)[p]
        if k in X_FIRST:
            n = X_FIRST.index(k)
            rows = half_rows(p)
            tb[k, slot, 0, xl, rows] = plus(tb.at[k, slot, 0, xl, rows], zf1.at[n, rows]).astype(BF)
            u_near(k, p, p).start()
        else:
            n = Z_FIRST.index(k)
            tb[k, slot, 1 - p] = plus(tb.at[k, slot, 1 - p], zf.at[n, p]).astype(BF)
            u_near(k, p, 1 - p).start()

    def u_turn(k):
        if k in X_FIRST:
            n = X_FIRST.index(k)
            for p in range(2):
                for a in range(2):
                    u_xnear(k, p, a).wait_recv()
            for i in range(4):
                tb[k, i, 0, xl] = plus(tb.at[k, i, 0, xl], xs4.at[n, 0, i], xs4.at[n, 1, i]).astype(BF)
            u_far(k, 0).start()
            u_far(k, 1).start()
            u_near(k, 0, 1).start()
            u_near(k, 1, 0).start()
        else:
            n = Z_FIRST.index(k)
            for p in range(2):
                for a in range(2):
                    u_near(k, p, a).wait_recv()
            for h, a in ((1, xl), (0, ol), (1, ol)):
                tb[k, z, h, a] = plus(tb.at[k, z, h, a], zn.at[n, 0, h, a], zn.at[n, 1, h, a]).astype(BF)
            u_xsend(k)

    def u_xpass(k, p):
        u_xfar(k, p).wait_recv()
        rows = half_rows(p)
        if k in X_FIRST:
            n = X_FIRST.index(k)
            for i in range(4):
                to = tb.at[k, i, 1 - p, ol, rows]
                to[...] = plus(to, xf4.at[n, i, rows]).astype(BF)
        else:
            n = Z_FIRST.index(k)
            to = tb.at[k, z, 1 - p, ol, rows]
            to[...] = plus(to, xf.at[n, rows]).astype(BF)
        u_xnear(k, 1 - p, p).start()

    def u_end(k):
        if k in X_FIRST:
            n = X_FIRST.index(k)
            for p in range(2):
                for a in range(2):
                    u_near(k, p, a).wait_recv()
            sum_out[k] = plus(tb.at[k, z, 0, xl], zs1.at[n, 0], zs1.at[n, 1])
        else:
            n = Z_FIRST.index(k)
            for p in range(2):
                for a in range(2):
                    u_xnear(k, p, a).wait_recv()
            sum_out[k] = plus(
                tb.at[k, z, 0, xl], zn.at[n, 0, 0, xl], zn.at[n, 1, 0, xl], xs.at[n, 0], xs.at[n, 1]
            )
        for p in range(2):
            u_far(k, p).wait_send()
            u_xfar(k, p).wait_send()
            for a in range(2):
                u_near(k, p, a).wait_send()
                u_xnear(k, p, a).wait_send()
        t_sent(k)

    def v_far(k, p):
        slot = (oh, xh)[p] * 4 + yo
        return rcopy(ib.at[k, slot], yf.at[k, p], vs.at[k, 1 + p], vr.at[k, 1 + p], d_y[p])

    def v_near(k, p, a):
        slot = (oh, xh)[a] * 4 + (yp, ym)[p]
        i = 3 + 2 * p + a
        return rcopy(ib.at[k, slot], yn.at[k, 2 * p + a], vs.at[k, i], vr.at[k, i], d_y[p])

    def v_last(k):
        return rcopy(ib.at[k, oh * 4 + y], xhb.at[k], vs.at[k, 7], vr.at[k, 7], d_xh)

    def part(k):
        w_core(k, 1 - c).wait_recv()

        def tile(j, carry):
            rows = pl.ds(pl.multiple_of(j * 256, 256), 256)
            left = wg[k].reshape(CD, HID)
            out = lax.dot_general(
                left, slope[rows, :], (((1,), (1,)), ((), ())), preferred_element_type=F32
            )
            out = (out * D ** (-0.5)).astype(BF)
            ib[k, 2 * j] = out[:, :128]
            ib[k, 2 * j + 1] = out[:, 128:]
            return carry

        lax.fori_loop(0, RT // 256, tile, 0)
        v_far(k, 0).start()
        v_far(k, 1).start()
        v_near(k, 0, 1).start()
        v_near(k, 1, 0).start()

    def v_pass(k, p):
        slot = (oh, xh)[p] * 4 + (yp, ym)[p]
        v_far(k, p).wait_recv()
        ib[k, slot] = plus(ib.at[k, slot], yf.at[k, p]).astype(BF)
        v_near(k, p, p).start()

    def v_cross(k):
        v_near(k, 0, 0).wait_recv()
        v_near(k, 1, 0).wait_recv()
        slot = oh * 4 + y
        ib[k, slot] = plus(ib.at[k, slot], yn.at[k, 0], yn.at[k, 2]).astype(BF)
        v_last(k).start()

    def v_end(k):
        v_near(k, 0, 1).wait_recv()
        v_near(k, 1, 1).wait_recv()
        v_last(k).wait_recv()
        ig_out[k] = plus(ib.at[k, s], xhb.at[k], yn.at[k, 1], yn.at[k, 3]).astype(BF)
        v_last(k).wait_send()
        for p in range(2):
            v_far(k, p).wait_send()
            v_near(k, p, 0).wait_send()
            v_near(k, p, 1).wait_send()
        w_sent(k)

    def both(work):
        return lambda k: work(k, 0), lambda k: work(k, 1)

    t_pass0, t_pass1 = both(t_pass)
    u_pass0, u_pass1 = both(u_pass)
    u_xpass0, u_xpass1 = both(u_xpass)
    v_pass0, v_pass1 = both(v_pass)
    term0, term1 = both(term)
    work = {
        T_OWN: t_own, T_PASS0: t_pass0, T_PASS1: t_pass1, T_SHARE: t_share,
        W_OWN: w_own, W_OTHER: w_other, W_PASS0: w_pass0, W_PASS1: w_pass1,
        W_SHARE: w_share, SLOPE0: slope0, SLOPE1: slope1, S_CROSS: s_cross,
        S_PASS: s_pass, TERM0: term0, TERM1: term1, U_PASS0: u_pass0,
        U_PASS1: u_pass1, U_TURN: u_turn, U_XPASS0: u_xpass0, U_XPASS1: u_xpass1,
        U_END: u_end, PART: part, V_PASS0: v_pass0, V_PASS1: v_pass1,
        V_CROSS: v_cross, V_END: v_end,
    }
    waited = False
    for name, k in ORDER:
        if name == W_OWN and not waited:
            get_mas.wait()
            waited = True
        work[name](k)
    s_sent()


def exchange(tokens, preact, cotangent, master):
    any_spec = pl.BlockSpec(memory_space=pl.ANY)
    dma = pltpu.SemaphoreType.DMA
    return pl.pallas_call(
        kernel,
        out_shape=(
            pltpu.VMEM((CH, RB, HID), F32),
            pltpu.VMEM((CH, CD, TOK), BF),
        ),
        in_specs=[any_spec] * 4,
        out_specs=(pl.BlockSpec(memory_space=pltpu.VMEM),) * 2,
        scratch_shapes=[
            pltpu.VMEM((CH, 4, 2, HALF, TOK), BF),
            pltpu.VMEM((CH, 4, HALF, TOK), BF),
            pltpu.VMEM((CH, 2, 8, RB, HID), BF),
            pltpu.VMEM((RT, HID), BF),
            pltpu.VMEM((3, HT, HID), BF),
            pltpu.VMEM((CH, 4, 2, 2, RB, HID), BF),
            pltpu.VMEM((len(Z_FIRST), 2, 2, RB, HID), BF),
            pltpu.VMEM((len(Z_FIRST), 2, 2, 2, RB, HID), BF),
            pltpu.VMEM((len(Z_FIRST), RB, HID), BF),
            pltpu.VMEM((len(Z_FIRST), 2, RB, HID), BF),
            pltpu.VMEM((len(X_FIRST), 4, RB, HID), BF),
            pltpu.VMEM((len(X_FIRST), 2, 4, RB, HID), BF),
            pltpu.VMEM((len(X_FIRST), RB, HID), BF),
            pltpu.VMEM((len(X_FIRST), 2, RB, HID), BF),
            pltpu.VMEM((CH, SEQS, CD, TOK), BF),
            pltpu.VMEM((CH, 2, CD, TOK), BF),
            pltpu.VMEM((CH, 4, CD, TOK), BF),
            pltpu.VMEM((CH, CD, TOK), BF),
            pltpu.VMEM((TOK, D), BF),
            pltpu.VMEM((CH, RB, HID), F32),
            pltpu.VMEM((2, STAGE, HID), BF),
            pltpu.VMEM((2, STAGE, HID), BF),
            dma((2,)),
            dma((2, 2)),
            dma((CH, 5)),
            dma((CH, 5)),
            dma((CH, 8)),
            dma((CH, 8)),
            dma((CH, 12)),
            dma((CH, 12)),
            dma((CH, 8)),
            dma((CH, 8)),
            dma((6,)),
            dma((6,)),
        ],
        compiler_params=pltpu.CompilerParams(
            collective_id=0, has_side_effects=True, vmem_limit_bytes=56 * 2**20
        ),
        cost_estimate=pl.CostEstimate(
            flops=4 * RT * HID * D, bytes_accessed=12 * 2**20, transcendentals=RT * HID
        ),
        name="exchange",
    )(tokens, preact, cotangent, master)


def finish_kernel(
    summed, turned, mas, first, second, new_mas, new_first, new_second, grad,
    insv, outv, gradv, in_sem, out_sem, grad_sem,
):
    def rows(k):
        return pl.ds(k * RB, RB)

    def get(k):
        srcs = (mas.at[rows(k)], first.at[rows(k)], second.at[rows(k)])
        return [pltpu.make_async_copy(src, insv.at[i, k], in_sem.at[i, k]) for i, src in enumerate(srcs)]

    def put(k):
        dsts = (new_mas, new_first, new_second)
        return [
            pltpu.make_async_copy(outv.at[i, k], dst.at[rows(k)], out_sem.at[i, k]) for i, dst in enumerate(dsts)
        ]

    put_grad = pltpu.make_async_copy(gradv, grad, grad_sem)
    for j in range(D // 128):
        pieces = []
        for m in range(128 // RB):
            q, row = place(j * 128 + m * RB)
            pieces.append(turned[q, row:row + RB, :])
        gradv[:, j * 128:(j + 1) * 128] = jnp.concatenate(pieces, axis=0).T
    put_grad.start()
    for k in range(CH):
        pseudo = summed[k] * (RT * REGIONS) ** (-0.5)
        one = 0.9 * first[rows(k), :] + 0.1 * pseudo
        two = 0.999 * second[rows(k), :] + 0.001 * pseudo * pseudo
        outv[0, k] = mas[rows(k), :] - 0.1 * one / (jnp.sqrt(two) + 0.001)
        outv[1, k] = one
        outv[2, k] = two
        for copy in put(k):
            copy.start()
    put_grad.wait()
    for k in range(CH):
        for copy in put(k):
            copy.wait()


def finish(summed, turned, master, first_moment, second_moment):
    any_spec = pl.BlockSpec(memory_space=pl.ANY)
    state = jax.ShapeDtypeStruct((OWN, HID), F32)
    dma = pltpu.SemaphoreType.DMA
    return pl.pallas_call(
        finish_kernel,
        out_shape=(state, state, state, jax.ShapeDtypeStruct((TOK, D), BF)),
        in_specs=[pl.BlockSpec(memory_space=pltpu.VMEM)] * 5,
        out_specs=(any_spec,) * 4,
        scratch_shapes=[
            pltpu.VMEM((3, CH, RB, HID), F32),
            pltpu.VMEM((3, CH, RB, HID), F32),
            pltpu.VMEM((TOK, D), BF),
            dma((3, CH)),
            dma((3, CH)),
            dma,
        ],
        compiler_params=pltpu.CompilerParams(vmem_limit_bytes=16 * 2**20),
        name="finish",
    )(summed, turned, master, first_moment, second_moment)


def per_device(tokens, preact, cotangent, master, first_moment, second_moment):
    summed, turned = exchange(tokens, preact, cotangent, master.reshape(CH, RB, HID))
    return finish(summed, turned, master, first_moment, second_moment)


def solution(mesh):
    block = P("region", "seq")
    rows = P(("region", "seq"), None)
    return jax.shard_map(
        per_device,
        mesh=mesh,
        in_specs=(rows, block, block, block, block, block),
        out_specs=(block, block, block, rows),
        check_vma=False,
    )
```

```python
import jax
import jax.numpy as jnp
from jax import lax
from jax.experimental import pallas as pl
from jax.experimental.pallas import tpu as pltpu
from jax.sharding import PartitionSpec as P

MESH = pl.DeviceIdType.MESH
BF = jnp.bfloat16
F32 = jnp.float32

D = 3584
REGIONS = 16
SEQS = 8
OWN = D // REGIONS
CH = 7
RB = OWN // CH
CD = D // CH
HALF = CD // 2
TOK = 128
HID = 1280
RT = TOK * SEQS
STAGE = 128
ST = RT // STAGE
HT = RT // 2
X_FIRST = (0, 2)
Z_FIRST = tuple(k for k in range(CH) if k not in X_FIRST)

(
    T_OWN, T_PASS0, T_PASS1, T_SHARE, W_OWN, W_OTHER, W_PASS0, W_PASS1, W_SHARE,
    SLOPE0, SLOPE1, S_CROSS, S_PASS, TERM0, TERM1, U_PASS0, U_PASS1, U_TURN,
    U_XPASS0, U_XPASS1, U_END, PART, V_PASS0, V_PASS1, V_CROSS, V_END,
) = range(26)
ORDER = (
    (W_OWN, 0), (W_OWN, 5), (W_OWN, 2), (T_OWN, 3), (SLOPE0, 0), (W_OWN, 6), (T_OWN, 1), (S_CROSS, 2),
    (W_OWN, 4), (SLOPE1, 0), (T_OWN, 6), (W_OTHER, 5), (T_OWN, 4), (W_PASS0, 5), (T_OWN, 2), (W_OTHER, 2),
    (T_PASS0, 6), (W_OTHER, 0), (W_PASS0, 2), (W_PASS1, 5), (W_OWN, 3), (T_PASS0, 1), (T_PASS0, 3),
    (T_PASS1, 6), (T_PASS1, 1), (W_PASS1, 2), (S_CROSS, 1), (W_OTHER, 6), (T_OWN, 5), (T_SHARE, 6),
    (S_CROSS, 0), (T_PASS1, 3), (W_OTHER, 4), (T_PASS0, 2), (W_PASS0, 0), (T_PASS0, 4), (T_OWN, 0),
    (T_PASS1, 2), (W_OTHER, 3), (W_SHARE, 5), (W_PASS1, 0), (T_SHARE, 3), (W_PASS1, 6), (W_PASS0, 4),
    (T_PASS1, 4), (S_CROSS, 3), (W_OWN, 1), (PART, 5), (W_SHARE, 2), (T_SHARE, 1), (TERM0, 6), (W_SHARE, 0),
    (T_SHARE, 4), (TERM0, 3), (W_PASS1, 4), (W_PASS0, 6), (T_PASS0, 5), (V_PASS0, 5), (PART, 2), (TERM0, 4),
    (W_PASS0, 1), (T_SHARE, 2), (PART, 0), (S_PASS, 0), (U_PASS1, 6), (TERM0, 1), (V_CROSS, 5),
    (W_OTHER, 1), (T_PASS1, 0), (W_SHARE, 6), (T_PASS1, 5), (W_PASS1, 3), (V_PASS1, 5), (W_SHARE, 4),
    (W_PASS0, 3), (T_PASS0, 0), (V_PASS0, 2), (TERM0, 2), (U_PASS1, 3), (TERM1, 2), (V_PASS0, 0),
    (TERM1, 3), (TERM1, 6), (T_SHARE, 0), (T_SHARE, 5), (TERM1, 1), (V_CROSS, 2), (W_SHARE, 3),
    (V_PASS1, 2), (U_XPASS0, 2), (U_XPASS1, 2), (PART, 6), (V_CROSS, 0), (TERM0, 0), (U_PASS0, 6),
    (TERM1, 0), (V_PASS1, 0), (V_PASS0, 6), (W_PASS1, 1), (U_PASS1, 1), (U_PASS0, 3), (PART, 3),
    (U_PASS0, 1), (TERM0, 5), (U_TURN, 6), (PART, 4), (U_XPASS1, 0), (W_SHARE, 1), (U_XPASS0, 0),
    (TERM1, 4), (V_PASS0, 3), (V_CROSS, 6), (U_TURN, 1), (U_XPASS0, 6), (U_XPASS1, 6), (V_PASS1, 3),
    (U_PASS1, 4), (TERM1, 5), (V_PASS1, 6), (U_TURN, 3), (V_PASS0, 4), (PART, 1), (U_PASS0, 4),
    (V_CROSS, 3), (U_XPASS0, 1), (U_PASS0, 5), (V_PASS1, 4), (V_END, 2), (U_XPASS1, 1), (U_PASS1, 5),
    (U_TURN, 0), (V_CROSS, 4), (U_TURN, 4), (V_PASS0, 1), (U_XPASS0, 3), (U_TURN, 2), (V_END, 3),
    (U_END, 6), (U_XPASS1, 3), (U_END, 1), (U_TURN, 5), (U_PASS1, 0), (U_PASS0, 0), (U_XPASS1, 4),
    (U_XPASS0, 4), (V_END, 0), (V_CROSS, 1), (V_PASS1, 1), (U_PASS0, 2), (V_END, 4), (U_XPASS1, 5),
    (U_PASS1, 2), (V_END, 6), (U_END, 3), (U_XPASS0, 5), (U_END, 2), (U_END, 4), (V_END, 5), (V_END, 1),
    (U_END, 0), (U_END, 5),
)

FIRST0 = next(k for name, k in ORDER if name == TERM0)
FIRST1 = next(k for name, k in ORDER if name == TERM1)


def place(d0):
    owner, rest = divmod(d0, OWN)
    k, i = divmod(rest, RB)
    xl, z, c = owner // 8, owner // 2 % 4, owner % 2
    return k, ((c * 4 + z) * 2 + xl) * RB + i


def rcopy(src, dst, send, recv, dev):
    return pltpu.make_async_remote_copy(
        src_ref=src, dst_ref=dst, send_sem=send, recv_sem=recv, device_id=dev, device_id_type=MESH
    )


def plus(*refs):
    total = refs[0][...].astype(F32)
    for ref in refs[1:]:
        total = total + ref[...].astype(F32)
    return total


def kernel(
    tok, pre, cot, mas, sum_out, ig_out,
    tg, tc, wg, slope, sx, tb, zf, zn, xf, xs, xf4, xs4, zf1, zs1, ib, yf, yn, xhb, tokv, masv, prev, cotv,
    in_sem, st_sem, ts, tr, ws, wr, us, ur, vs, vr, ss, sr,
):
    r = lax.axis_index("region")
    s = lax.axis_index("seq")
    xl, z, c = r // 8, (r // 2) % 4, r % 2
    xh, y = s // 4, s % 4
    ol, oh = 1 - xl, 1 - xh
    zp, zm, zo = (z + 1) % 4, (z + 3) % 4, (z + 2) % 4
    yp, ym, yo = (y + 1) % 4, (y + 3) % 4, (y + 2) % 4

    def device(a, b, d, e, f):
        return (a * 8 + b * 2 + d, e * 4 + f)

    d_core = device(xl, z, 1 - c, xh, y)
    d_x = (device(ol, z, c, xh, y), device(ol, z, c, oh, y))
    d_xh = device(xl, z, c, oh, y)
    d_z = (device(xl, zp, c, xh, y), device(xl, zm, c, xh, y))
    d_y = (device(xl, z, c, xh, yp), device(xl, z, c, xh, ym))

    get_tok = pltpu.make_async_copy(tok, tokv, in_sem.at[0])
    get_mas = pltpu.make_async_copy(mas, masv, in_sem.at[1])
    get_tok.start()
    get_mas.start()

    def stage(i, slot):
        half = oh + (i // 4) * (xh - oh)
        rows = pl.ds(pl.multiple_of((half * 4 + i % 4) * STAGE, STAGE), STAGE)
        return rows, (
            pltpu.make_async_copy(pre.at[rows], prev.at[slot], st_sem.at[0, slot]),
            pltpu.make_async_copy(cot.at[rows], cotv.at[slot], st_sem.at[1, slot]),
        )

    for i in range(2):
        for copy in stage(i, i)[1]:
            copy.start()

    barrier = pltpu.get_barrier_semaphore()
    for dev in (d_core, *d_x, d_xh, *d_z, *d_y):
        pl.semaphore_signal(barrier, inc=1, device_id=dev, device_id_type=MESH)

    get_tok.wait()
    for j in range(D // 128):
        turned = tokv[:, j * 128:(j + 1) * 128].T
        for m in range(128 // RB):
            k, row = place(j * 128 + m * RB)
            half, row = divmod(row, HALF)
            tg[k, y, half, row:row + RB, :] = turned[m * RB:(m + 1) * RB, :]
    pl.semaphore_wait(barrier, 8)

    def t_copy(k, slot, i):
        return rcopy(tg.at[k, slot], tg.at[k, slot], ts.at[k, i], tr.at[k, i], d_y[i])

    def t_half(k, slot, p):
        return rcopy(tg.at[k, slot, p], tg.at[k, slot, p], ts.at[k, 2 + p], tr.at[k, 2 + p], d_y[p])

    def t_core(k):
        return rcopy(tg.at[k, :, 1 - c], tc.at[k], ts.at[k, 4], tr.at[k, 4], d_core)

    def t_own(k):
        t_copy(k, y, 0).start()
        t_copy(k, y, 1).start()

    def t_pass(k, p):
        t_copy(k, y, p).wait_recv()
        t_half(k, (ym, yp)[p], p).start()

    def t_share(k):
        t_half(k, yo, 0).wait_recv()
        t_half(k, yo, 1).wait_recv()
        t_core(k).start()

    def t_sent(k):
        for p in range(2):
            t_copy(k, y, p).wait_send()
            t_half(k, y, p).wait_send()
        t_core(k).wait_send()

    def w_copy(k, slot, i, dev):
        return rcopy(wg.at[k, c, slot], wg.at[k, c, slot], ws.at[k, i], wr.at[k, i], dev)

    def w_core(k, half):
        return rcopy(wg.at[k, half], wg.at[k, half], ws.at[k, 7], wr.at[k, 7], d_core)

    def w_wait(k, *ids):
        for i in ids:
            w_copy(k, 0, i, d_x[0]).wait_recv()

    def w_own(k):
        wg[k, c, z * 2 + xl] = masv[k].astype(BF)
        w_copy(k, z * 2 + xl, 0, d_x[0]).start()
        w_copy(k, z * 2 + xl, 1, d_z[0]).start()
        w_copy(k, z * 2 + xl, 3, d_z[1]).start()

    def w_other(k):
        w_wait(k, 0)
        w_copy(k, z * 2 + ol, 2, d_z[0]).start()
        w_copy(k, z * 2 + ol, 4, d_z[1]).start()

    def w_pass0(k):
        w_wait(k, 1)
        w_copy(k, zm * 2 + xl, 5, d_z[0]).start()

    def w_pass1(k):
        w_wait(k, 4)
        w_copy(k, zp * 2 + ol, 6, d_z[1]).start()

    def w_share(k):
        w_wait(k, 3, 2, 5, 6)
        w_core(k, c).start()

    def w_sent(k):
        for i in range(7):
            w_copy(k, 0, i, d_x[0]).wait_send()
        w_core(k, c).wait_send()

    def make_slope(i, carry):
        slot = i % 2
        rows, copies = stage(i, slot)
        for copy in copies:
            copy.wait()
        lin = prev[slot].astype(F32)
        sig = jax.nn.sigmoid(lin)
        slope[rows, :] = (cotv[slot].astype(F32) * sig * (1.0 + lin * (1.0 - sig))).astype(BF)

        @pl.when(i + 2 < ST)
        def _():
            for copy in stage(i + 2, slot)[1]:
                copy.start()

        return carry

    def own_rows():
        return pl.ds(pl.multiple_of(xh * HT, HT), HT)

    def s_copy(i):
        rows = pl.ds(pl.multiple_of((oh * 4 + i) * STAGE, STAGE), STAGE)
        return rcopy(slope.at[rows], sx.at[0, pl.ds(i * STAGE, STAGE)], ss.at[i], sr.at[i], d_xh)

    def s_core(i):
        src = (slope.at[own_rows()], sx.at[0])[i]
        return rcopy(src, sx.at[1 + i], ss.at[4 + i], sr.at[4 + i], d_core)

    def slope0(k):
        lax.fori_loop(0, ST // 2, make_slope, 0)

    def slope1(k):
        lax.fori_loop(ST // 2, ST, make_slope, 0)
        s_core(0).start()

    def s_cross(i):
        s_copy(i).start()

    def s_pass(k):
        for i in range(4):
            s_copy(i).wait_recv()
        s_core(1).start()

    def s_sent():
        for i in range(4):
            s_copy(i).wait_send()
        s_core(0).wait_send()
        s_core(1).wait_send()

    def u_copy(k, i, src, dst, dev):
        return rcopy(src, dst, us.at[k, i], ur.at[k, i], dev)

    def half_rows(a):
        return pl.ds(a * (RB // 2), RB // 2)

    def u_far(k, p):
        if k in X_FIRST:
            n = X_FIRST.index(k)
            src, dst = tb.at[k, zo, 0, xl, half_rows(p)], zf1.at[n, half_rows(p)]
        else:
            n = Z_FIRST.index(k)
            src, dst = tb.at[k, zo, 1 - p], zf.at[n, p]
        return u_copy(k, p, src, dst, d_z[p])

    def u_near(k, p, a):
        slot = (zp, zm)[p]
        if k in X_FIRST:
            n = X_FIRST.index(k)
            src, dst = tb.at[k, slot, 0, xl, half_rows(a)], zs1.at[n, p, half_rows(a)]
        else:
            n = Z_FIRST.index(k)
            src, dst = tb.at[k, slot, a], zn.at[n, p, a]
        return u_copy(k, 2 + 2 * p + a, src, dst, d_z[p])

    def u_xfar(k, p):
        if k in X_FIRST:
            n = X_FIRST.index(k)
            src, dst = tb.at[k, :, 1, xl, half_rows(p)], xf4.at[n, :, half_rows(p)]
        else:
            n = Z_FIRST.index(k)
            src, dst = tb.at[k, z, 1, xl, half_rows(p)], xf.at[n, half_rows(p)]
        return u_copy(k, 6 + p, src, dst, d_x[p])

    def u_xnear(k, p, a):
        if k in X_FIRST:
            n = X_FIRST.index(k)
            src, dst = tb.at[k, :, p, ol, half_rows(a)], xs4.at[n, p, :, half_rows(a)]
        else:
            n = Z_FIRST.index(k)
            src, dst = tb.at[k, z, p, ol, half_rows(a)], xs.at[n, p, half_rows(a)]
        return u_copy(k, 8 + 2 * p + a, src, dst, d_x[p])

    def term(k, h):
        if h == 0:
            t_core(k).wait_recv()
            if k == FIRST0:
                s_core(0).wait_recv()
        elif k == FIRST1:
            s_core(1).wait_recv()

        def tile(j, carry):
            cols = pl.ds(pl.multiple_of(j * 256, 256), 256)
            mine = jnp.concatenate([tg[k, i, c] for i in range(4)], axis=1)
            theirs = jnp.concatenate([tc[k, i] for i in range(4)], axis=1)
            own = slope[own_rows(), cols] if h == 0 else sx[0, :, cols]
            out = jnp.dot(mine, own, preferred_element_type=F32)
            out = out + jnp.dot(theirs, sx[1 + h, :, cols], preferred_element_type=F32)
            tb[k, :, h, :, :, cols] = out.astype(BF).reshape(4, 2, RB, 256)
            return carry

        lax.fori_loop(0, HID // 256, tile, 0)
        if k in Z_FIRST:
            u_far(k, 1 - h).start()
            u_near(k, h, h).start()
        elif h == 1:
            u_xsend(k)

    def u_xsend(k):
        u_xfar(k, 0).start()
        u_xfar(k, 1).start()
        u_xnear(k, 0, 0).start()
        u_xnear(k, 1, 1).start()

    def u_pass(k, p):
        u_far(k, p).wait_recv()
        slot = (zp, zm)[p]
        if k in X_FIRST:
            n = X_FIRST.index(k)
            rows = half_rows(p)
            tb[k, slot, 0, xl, rows] = plus(tb.at[k, slot, 0, xl, rows], zf1.at[n, rows]).astype(BF)
            u_near(k, p, p).start()
        else:
            n = Z_FIRST.index(k)
            tb[k, slot, 1 - p] = plus(tb.at[k, slot, 1 - p], zf.at[n, p]).astype(BF)
            u_near(k, p, 1 - p).start()

    def u_turn(k):
        if k in X_FIRST:
            n = X_FIRST.index(k)
            for p in range(2):
                for a in range(2):
                    u_xnear(k, p, a).wait_recv()
            for i in range(4):
                tb[k, i, 0, xl] = plus(tb.at[k, i, 0, xl], xs4.at[n, 0, i], xs4.at[n, 1, i]).astype(BF)
            u_far(k, 0).start()
            u_far(k, 1).start()
            u_near(k, 0, 1).start()
            u_near(k, 1, 0).start()
        else:
            n = Z_FIRST.index(k)
            for p in range(2):
                for a in range(2):
                    u_near(k, p, a).wait_recv()
            for h, a in ((1, xl), (0, ol), (1, ol)):
                tb[k, z, h, a] = plus(tb.at[k, z, h, a], zn.at[n, 0, h, a], zn.at[n, 1, h, a]).astype(BF)
            u_xsend(k)

    def u_xpass(k, p):
        u_xfar(k, p).wait_recv()
        rows = half_rows(p)
        if k in X_FIRST:
            n = X_FIRST.index(k)
            for i in range(4):
                to = tb.at[k, i, 1 - p, ol, rows]
                to[...] = plus(to, xf4.at[n, i, rows]).astype(BF)
        else:
            n = Z_FIRST.index(k)
            to = tb.at[k, z, 1 - p, ol, rows]
            to[...] = plus(to, xf.at[n, rows]).astype(BF)
        u_xnear(k, 1 - p, p).start()

    def u_end(k):
        if k in X_FIRST:
            n = X_FIRST.index(k)
            for p in range(2):
                for a in range(2):
                    u_near(k, p, a).wait_recv()
            sum_out[k] = plus(tb.at[k, z, 0, xl], zs1.at[n, 0], zs1.at[n, 1])
        else:
            n = Z_FIRST.index(k)
            for p in range(2):
                for a in range(2):
                    u_xnear(k, p, a).wait_recv()
            sum_out[k] = plus(
                tb.at[k, z, 0, xl], zn.at[n, 0, 0, xl], zn.at[n, 1, 0, xl], xs.at[n, 0], xs.at[n, 1]
            )
        for p in range(2):
            u_far(k, p).wait_send()
            u_xfar(k, p).wait_send()
            for a in range(2):
                u_near(k, p, a).wait_send()
                u_xnear(k, p, a).wait_send()
        t_sent(k)

    def v_far(k, p):
        slot = (oh, xh)[p] * 4 + yo
        return rcopy(ib.at[k, slot], yf.at[k, p], vs.at[k, 1 + p], vr.at[k, 1 + p], d_y[p])

    def v_near(k, p, a):
        slot = (oh, xh)[a] * 4 + (yp, ym)[p]
        i = 3 + 2 * p + a
        return rcopy(ib.at[k, slot], yn.at[k, 2 * p + a], vs.at[k, i], vr.at[k, i], d_y[p])

    def v_last(k):
        return rcopy(ib.at[k, oh * 4 + y], xhb.at[k], vs.at[k, 7], vr.at[k, 7], d_xh)

    def part(k):
        w_core(k, 1 - c).wait_recv()

        def tile(j, carry):
            rows = pl.ds(pl.multiple_of(j * 256, 256), 256)
            left = wg[k].reshape(CD, HID)
            out = lax.dot_general(
                left, slope[rows, :], (((1,), (1,)), ((), ())), preferred_element_type=F32
            )
            out = (out * D ** (-0.5)).astype(BF)
            ib[k, 2 * j] = out[:, :128]
            ib[k, 2 * j + 1] = out[:, 128:]
            return carry

        lax.fori_loop(0, RT // 256, tile, 0)
        v_far(k, 0).start()
        v_far(k, 1).start()
        v_near(k, 0, 1).start()
        v_near(k, 1, 0).start()

    def v_pass(k, p):
        slot = (oh, xh)[p] * 4 + (yp, ym)[p]
        v_far(k, p).wait_recv()
        ib[k, slot] = plus(ib.at[k, slot], yf.at[k, p]).astype(BF)
        v_near(k, p, p).start()

    def v_cross(k):
        v_near(k, 0, 0).wait_recv()
        v_near(k, 1, 0).wait_recv()
        slot = oh * 4 + y
        ib[k, slot] = plus(ib.at[k, slot], yn.at[k, 0], yn.at[k, 2]).astype(BF)
        v_last(k).start()

    def v_end(k):
        v_near(k, 0, 1).wait_recv()
        v_near(k, 1, 1).wait_recv()
        v_last(k).wait_recv()
        ig_out[k] = plus(ib.at[k, s], xhb.at[k], yn.at[k, 1], yn.at[k, 3]).astype(BF)
        v_last(k).wait_send()
        for p in range(2):
            v_far(k, p).wait_send()
            v_near(k, p, 0).wait_send()
            v_near(k, p, 1).wait_send()
        w_sent(k)

    def both(work):
        return lambda k: work(k, 0), lambda k: work(k, 1)

    t_pass0, t_pass1 = both(t_pass)
    u_pass0, u_pass1 = both(u_pass)
    u_xpass0, u_xpass1 = both(u_xpass)
    v_pass0, v_pass1 = both(v_pass)
    term0, term1 = both(term)
    work = {
        T_OWN: t_own, T_PASS0: t_pass0, T_PASS1: t_pass1, T_SHARE: t_share,
        W_OWN: w_own, W_OTHER: w_other, W_PASS0: w_pass0, W_PASS1: w_pass1,
        W_SHARE: w_share, SLOPE0: slope0, SLOPE1: slope1, S_CROSS: s_cross,
        S_PASS: s_pass, TERM0: term0, TERM1: term1, U_PASS0: u_pass0,
        U_PASS1: u_pass1, U_TURN: u_turn, U_XPASS0: u_xpass0, U_XPASS1: u_xpass1,
        U_END: u_end, PART: part, V_PASS0: v_pass0, V_PASS1: v_pass1,
        V_CROSS: v_cross, V_END: v_end,
    }
    waited = False
    for name, k in ORDER:
        if name == W_OWN and not waited:
            get_mas.wait()
            waited = True
        work[name](k)
    s_sent()


def exchange(tokens, preact, cotangent, master):
    any_spec = pl.BlockSpec(memory_space=pl.ANY)
    dma = pltpu.SemaphoreType.DMA
    return pl.pallas_call(
        kernel,
        out_shape=(
            pltpu.VMEM((CH, RB, HID), F32),
            pltpu.VMEM((CH, CD, TOK), BF),
        ),
        in_specs=[any_spec] * 4,
        out_specs=(pl.BlockSpec(memory_space=pltpu.VMEM),) * 2,
        scratch_shapes=[
            pltpu.VMEM((CH, 4, 2, HALF, TOK), BF),
            pltpu.VMEM((CH, 4, HALF, TOK), BF),
            pltpu.VMEM((CH, 2, 8, RB, HID), BF),
            pltpu.VMEM((RT, HID), BF),
            pltpu.VMEM((3, HT, HID), BF),
            pltpu.VMEM((CH, 4, 2, 2, RB, HID), BF),
            pltpu.VMEM((len(Z_FIRST), 2, 2, RB, HID), BF),
            pltpu.VMEM((len(Z_FIRST), 2, 2, 2, RB, HID), BF),
            pltpu.VMEM((len(Z_FIRST), RB, HID), BF),
            pltpu.VMEM((len(Z_FIRST), 2, RB, HID), BF),
            pltpu.VMEM((len(X_FIRST), 4, RB, HID), BF),
            pltpu.VMEM((len(X_FIRST), 2, 4, RB, HID), BF),
            pltpu.VMEM((len(X_FIRST), RB, HID), BF),
            pltpu.VMEM((len(X_FIRST), 2, RB, HID), BF),
            pltpu.VMEM((CH, SEQS, CD, TOK), BF),
            pltpu.VMEM((CH, 2, CD, TOK), BF),
            pltpu.VMEM((CH, 4, CD, TOK), BF),
            pltpu.VMEM((CH, CD, TOK), BF),
            pltpu.VMEM((TOK, D), BF),
            pltpu.VMEM((CH, RB, HID), F32),
            pltpu.VMEM((2, STAGE, HID), BF),
            pltpu.VMEM((2, STAGE, HID), BF),
            dma((2,)),
            dma((2, 2)),
            dma((CH, 5)),
            dma((CH, 5)),
            dma((CH, 8)),
            dma((CH, 8)),
            dma((CH, 12)),
            dma((CH, 12)),
            dma((CH, 8)),
            dma((CH, 8)),
            dma((6,)),
            dma((6,)),
        ],
        compiler_params=pltpu.CompilerParams(
            collective_id=0, has_side_effects=True, vmem_limit_bytes=56 * 2**20
        ),
        cost_estimate=pl.CostEstimate(
            flops=4 * RT * HID * D, bytes_accessed=12 * 2**20, transcendentals=RT * HID
        ),
        name="exchange",
    )(tokens, preact, cotangent, master)


def finish_kernel(
    summed, turned, mas, first, second, new_mas, new_first, new_second, grad,
    insv, outv, gradv, in_sem, out_sem, grad_sem,
):
    def rows(k):
        return pl.ds(k * RB, RB)

    def get(k):
        srcs = (mas.at[rows(k)], first.at[rows(k)], second.at[rows(k)])
        return [pltpu.make_async_copy(src, insv.at[i, k], in_sem.at[i, k]) for i, src in enumerate(srcs)]

    def put(k):
        dsts = (new_mas, new_first, new_second)
        return [
            pltpu.make_async_copy(outv.at[i, k], dst.at[rows(k)], out_sem.at[i, k]) for i, dst in enumerate(dsts)
        ]

    put_grad = pltpu.make_async_copy(gradv, grad, grad_sem)
    for j in range(D // 128):
        pieces = []
        for m in range(128 // RB):
            q, row = place(j * 128 + m * RB)
            pieces.append(turned[q, row:row + RB, :])
        gradv[:, j * 128:(j + 1) * 128] = jnp.concatenate(pieces, axis=0).T
    put_grad.start()
    for k in range(CH):
        pseudo = summed[k] * (RT * REGIONS) ** (-0.5)
        one = 0.9 * first[rows(k), :] + 0.1 * pseudo
        two = 0.999 * second[rows(k), :] + 0.001 * pseudo * pseudo
        outv[0, k] = mas[rows(k), :] - 0.1 * one / (jnp.sqrt(two) + 0.001)
        outv[1, k] = one
        outv[2, k] = two
        for copy in put(k):
            copy.start()
    put_grad.wait()
    for k in range(CH):
        for copy in put(k):
            copy.wait()


def finish(summed, turned, master, first_moment, second_moment):
    any_spec = pl.BlockSpec(memory_space=pl.ANY)
    state = jax.ShapeDtypeStruct((OWN, HID), F32)
    dma = pltpu.SemaphoreType.DMA
    return pl.pallas_call(
        finish_kernel,
        out_shape=(state, state, state, jax.ShapeDtypeStruct((TOK, D), BF)),
        in_specs=[pl.BlockSpec(memory_space=pltpu.VMEM)] * 5,
        out_specs=(any_spec,) * 4,
        scratch_shapes=[
            pltpu.VMEM((3, CH, RB, HID), F32),
            pltpu.VMEM((3, CH, RB, HID), F32),
            pltpu.VMEM((TOK, D), BF),
            dma((3, CH)),
            dma((3, CH)),
            dma,
        ],
        compiler_params=pltpu.CompilerParams(vmem_limit_bytes=16 * 2**20),
        name="finish",
    )(summed, turned, master, first_moment, second_moment)


def per_device(tokens, preact, cotangent, master, first_moment, second_moment):
    summed, turned = exchange(tokens, preact, cotangent, master.reshape(CH, RB, HID))
    return finish(summed, turned, master, first_moment, second_moment)


def solution(mesh):
    block = P("region", "seq")
    rows = P(("region", "seq"), None)
    return jax.shard_map(
        per_device,
        mesh=mesh,
        in_specs=(rows, block, block, block, block, block),
        out_specs=(block, block, block, rows),
        check_vma=False,
    )
```

```python
import jax
import jax.numpy as jnp
from jax import lax
from jax.experimental import pallas as pl
from jax.experimental.pallas import tpu as pltpu
from jax.sharding import PartitionSpec as P

MESH = pl.DeviceIdType.MESH
BF = jnp.bfloat16
F32 = jnp.float32

D = 3584
REGIONS = 16
SEQS = 8
OWN = D // REGIONS
CH = 7
RB = OWN // CH
CD = D // CH
HALF = CD // 2
TOK = 128
HID = 1280
RT = TOK * SEQS
STAGE = 128
ST = RT // STAGE
HT = RT // 2
X_FIRST = (0, 2)
Z_FIRST = tuple(k for k in range(CH) if k not in X_FIRST)

(
    T_OWN, T_PASS0, T_PASS1, T_SHARE, W_OWN, W_OTHER, W_PASS0, W_PASS1, W_SHARE,
    SLOPE0, SLOPE1, S_CROSS, S_PASS, TERM0, TERM1, U_PASS0, U_PASS1, U_TURN,
    U_XPASS0, U_XPASS1, U_END, PART, V_PASS0, V_PASS1, V_CROSS, V_END,
) = range(26)
ORDER = (
    (W_OWN, 0), (W_OWN, 5), (W_OWN, 2), (T_OWN, 3), (SLOPE0, 0), (W_OWN, 6), (T_OWN, 1), (S_CROSS, 2),
    (W_OWN, 4), (SLOPE1, 0), (T_OWN, 6), (W_OTHER, 5), (T_OWN, 4), (W_PASS0, 5), (T_OWN, 2), (W_OTHER, 2),
    (T_PASS0, 6), (W_OTHER, 0), (W_PASS0, 2), (W_PASS1, 5), (W_OWN, 3), (T_PASS0, 1), (T_PASS0, 3),
    (T_PASS1, 6), (T_PASS1, 1), (W_PASS1, 2), (S_CROSS, 1), (W_OTHER, 6), (T_OWN, 5), (T_SHARE, 6),
    (S_CROSS, 0), (T_PASS1, 3), (W_OTHER, 4), (T_PASS0, 2), (W_PASS0, 0), (T_PASS0, 4), (T_OWN, 0),
    (T_PASS1, 2), (W_OTHER, 3), (W_SHARE, 5), (W_PASS1, 0), (T_SHARE, 3), (W_PASS1, 6), (W_PASS0, 4),
    (T_PASS1, 4), (S_CROSS, 3), (W_OWN, 1), (PART, 5), (W_SHARE, 2), (T_SHARE, 1), (TERM0, 6), (W_SHARE, 0),
    (T_SHARE, 4), (TERM0, 3), (W_PASS1, 4), (W_PASS0, 6), (T_PASS0, 5), (V_PASS0, 5), (PART, 2), (TERM0, 4),
    (W_PASS0, 1), (T_SHARE, 2), (PART, 0), (S_PASS, 0), (U_PASS1, 6), (TERM0, 1), (V_CROSS, 5),
    (W_OTHER, 1), (T_PASS1, 0), (W_SHARE, 6), (T_PASS1, 5), (W_PASS1, 3), (V_PASS1, 5), (W_SHARE, 4),
    (W_PASS0, 3), (T_PASS0, 0), (V_PASS0, 2), (TERM0, 2), (U_PASS1, 3), (TERM1, 2), (V_PASS0, 0),
    (TERM1, 3), (TERM1, 6), (T_SHARE, 0), (T_SHARE, 5), (TERM1, 1), (V_CROSS, 2), (W_SHARE, 3),
    (V_PASS1, 2), (U_XPASS0, 2), (U_XPASS1, 2), (PART, 6), (V_CROSS, 0), (TERM0, 0), (U_PASS0, 6),
    (TERM1, 0), (V_PASS1, 0), (V_PASS0, 6), (W_PASS1, 1), (U_PASS1, 1), (U_PASS0, 3), (PART, 3),
    (U_PASS0, 1), (TERM0, 5), (U_TURN, 6), (PART, 4), (U_XPASS1, 0), (W_SHARE, 1), (U_XPASS0, 0),
    (TERM1, 4), (V_PASS0, 3), (V_CROSS, 6), (U_TURN, 1), (U_XPASS0, 6), (U_XPASS1, 6), (V_PASS1, 3),
    (U_PASS1, 4), (TERM1, 5), (V_PASS1, 6), (U_TURN, 3), (V_PASS0, 4), (PART, 1), (U_PASS0, 4),
    (V_CROSS, 3), (U_XPASS0, 1), (U_PASS0, 5), (V_PASS1, 4), (V_END, 2), (U_XPASS1, 1), (U_PASS1, 5),
    (U_TURN, 0), (V_CROSS, 4), (U_TURN, 4), (V_PASS0, 1), (U_XPASS0, 3), (U_TURN, 2), (V_END, 3),
    (U_END, 6), (U_XPASS1, 3), (U_END, 1), (U_TURN, 5), (U_PASS1, 0), (U_PASS0, 0), (U_XPASS1, 4),
    (U_XPASS0, 4), (V_END, 0), (V_CROSS, 1), (V_PASS1, 1), (U_PASS0, 2), (V_END, 4), (U_XPASS1, 5),
    (U_PASS1, 2), (V_END, 6), (U_END, 3), (U_XPASS0, 5), (U_END, 2), (U_END, 4), (V_END, 5), (V_END, 1),
    (U_END, 0), (U_END, 5),
)

FIRST0 = next(k for name, k in ORDER if name == TERM0)
FIRST1 = next(k for name, k in ORDER if name == TERM1)


def place(d0):
    owner, rest = divmod(d0, OWN)
    k, i = divmod(rest, RB)
    xl, z, c = owner // 8, owner // 2 % 4, owner % 2
    return k, ((c * 4 + z) * 2 + xl) * RB + i


def rcopy(src, dst, send, recv, dev):
    return pltpu.make_async_remote_copy(
        src_ref=src, dst_ref=dst, send_sem=send, recv_sem=recv, device_id=dev, device_id_type=MESH
    )


def plus(*refs):
    total = refs[0][...].astype(F32)
    for ref in refs[1:]:
        total = total + ref[...].astype(F32)
    return total


def kernel(
    tok, pre, cot, mas, first, second, new_mas, new_first, new_second, ig_out,
    tg, tc, wg, slope, sx, tb, zf, zn, xf, xs, xf4, xs4, zf1, zs1, ib, yf, yn, xhb, tokv, prev, cotv,
    in_sem, st_sem, ts, tr, ws, wr, us, ur, vs, vr, ss, sr,
):
    r = lax.axis_index("region")
    s = lax.axis_index("seq")
    xl, z, c = r // 8, (r // 2) % 4, r % 2
    xh, y = s // 4, s % 4
    ol, oh = 1 - xl, 1 - xh
    zp, zm, zo = (z + 1) % 4, (z + 3) % 4, (z + 2) % 4
    yp, ym, yo = (y + 1) % 4, (y + 3) % 4, (y + 2) % 4

    def device(a, b, d, e, f):
        return (a * 8 + b * 2 + d, e * 4 + f)

    d_core = device(xl, z, 1 - c, xh, y)
    d_x = (device(ol, z, c, xh, y), device(ol, z, c, oh, y))
    d_xh = device(xl, z, c, oh, y)
    d_z = (device(xl, zp, c, xh, y), device(xl, zm, c, xh, y))
    d_y = (device(xl, z, c, xh, yp), device(xl, z, c, xh, ym))

    get_tok = pltpu.make_async_copy(tok, tokv, in_sem.at[0])
    get_mas = pltpu.make_async_copy(mas, new_mas, in_sem.at[1])
    get_first = pltpu.make_async_copy(first, new_first, in_sem.at[2])
    get_second = pltpu.make_async_copy(second, new_second, in_sem.at[3])
    get_tok.start()
    get_mas.start()

    def stage(i, slot):
        half = oh + (i // 4) * (xh - oh)
        rows = pl.ds(pl.multiple_of((half * 4 + i % 4) * STAGE, STAGE), STAGE)
        return rows, (
            pltpu.make_async_copy(pre.at[rows], prev.at[slot], st_sem.at[0, slot]),
            pltpu.make_async_copy(cot.at[rows], cotv.at[slot], st_sem.at[1, slot]),
        )

    for i in range(2):
        for copy in stage(i, i)[1]:
            copy.start()

    barrier = pltpu.get_barrier_semaphore()
    for dev in (d_core, *d_x, d_xh, *d_z, *d_y):
        pl.semaphore_signal(barrier, inc=1, device_id=dev, device_id_type=MESH)

    get_tok.wait()
    for j in range(D // 128):
        turned = tokv[:, j * 128:(j + 1) * 128].T
        for m in range(128 // RB):
            k, row = place(j * 128 + m * RB)
            half, row = divmod(row, HALF)
            tg[k, y, half, row:row + RB, :] = turned[m * RB:(m + 1) * RB, :]
    get_first.start()
    get_second.start()
    pl.semaphore_wait(barrier, 8)

    def t_copy(k, slot, i):
        return rcopy(tg.at[k, slot], tg.at[k, slot], ts.at[k, i], tr.at[k, i], d_y[i])

    def t_half(k, slot, p):
        return rcopy(tg.at[k, slot, p], tg.at[k, slot, p], ts.at[k, 2 + p], tr.at[k, 2 + p], d_y[p])

    def t_core(k):
        return rcopy(tg.at[k, :, 1 - c], tc.at[k], ts.at[k, 4], tr.at[k, 4], d_core)

    def t_own(k):
        t_copy(k, y, 0).start()
        t_copy(k, y, 1).start()

    def t_pass(k, p):
        t_copy(k, y, p).wait_recv()
        t_half(k, (ym, yp)[p], p).start()

    def t_share(k):
        t_half(k, yo, 0).wait_recv()
        t_half(k, yo, 1).wait_recv()
        t_core(k).start()

    def t_sent(k):
        for p in range(2):
            t_copy(k, y, p).wait_send()
            t_half(k, y, p).wait_send()
        t_core(k).wait_send()

    def w_copy(k, slot, i, dev):
        return rcopy(wg.at[k, c, slot], wg.at[k, c, slot], ws.at[k, i], wr.at[k, i], dev)

    def w_core(k, half):
        return rcopy(wg.at[k, half], wg.at[k, half], ws.at[k, 7], wr.at[k, 7], d_core)

    def w_wait(k, *ids):
        for i in ids:
            w_copy(k, 0, i, d_x[0]).wait_recv()

    def w_own(k):
        wg[k, c, z * 2 + xl] = new_mas[k].astype(BF)
        w_copy(k, z * 2 + xl, 0, d_x[0]).start()
        w_copy(k, z * 2 + xl, 1, d_z[0]).start()
        w_copy(k, z * 2 + xl, 3, d_z[1]).start()

    def w_other(k):
        w_wait(k, 0)
        w_copy(k, z * 2 + ol, 2, d_z[0]).start()
        w_copy(k, z * 2 + ol, 4, d_z[1]).start()

    def w_pass0(k):
        w_wait(k, 1)
        w_copy(k, zm * 2 + xl, 5, d_z[0]).start()

    def w_pass1(k):
        w_wait(k, 4)
        w_copy(k, zp * 2 + ol, 6, d_z[1]).start()

    def w_share(k):
        w_wait(k, 3, 2, 5, 6)
        w_core(k, c).start()

    def w_sent(k):
        for i in range(7):
            w_copy(k, 0, i, d_x[0]).wait_send()
        w_core(k, c).wait_send()

    def make_slope(i, carry):
        slot = i % 2
        rows, copies = stage(i, slot)
        for copy in copies:
            copy.wait()
        lin = prev[slot].astype(F32)
        sig = jax.nn.sigmoid(lin)
        slope[rows, :] = (cotv[slot].astype(F32) * sig * (1.0 + lin * (1.0 - sig))).astype(BF)

        @pl.when(i + 2 < ST)
        def _():
            for copy in stage(i + 2, slot)[1]:
                copy.start()

        return carry

    def own_rows():
        return pl.ds(pl.multiple_of(xh * HT, HT), HT)

    def s_copy(i):
        rows = pl.ds(pl.multiple_of((oh * 4 + i) * STAGE, STAGE), STAGE)
        return rcopy(slope.at[rows], sx.at[0, pl.ds(i * STAGE, STAGE)], ss.at[i], sr.at[i], d_xh)

    def s_core(i):
        src = (slope.at[own_rows()], sx.at[0])[i]
        return rcopy(src, sx.at[1 + i], ss.at[4 + i], sr.at[4 + i], d_core)

    def slope0(k):
        lax.fori_loop(0, ST // 2, make_slope, 0)

    def slope1(k):
        lax.fori_loop(ST // 2, ST, make_slope, 0)
        s_core(0).start()

    def s_cross(i):
        s_copy(i).start()

    def s_pass(k):
        for i in range(4):
            s_copy(i).wait_recv()
        s_core(1).start()

    def s_sent():
        for i in range(4):
            s_copy(i).wait_send()
        s_core(0).wait_send()
        s_core(1).wait_send()

    def u_copy(k, i, src, dst, dev):
        return rcopy(src, dst, us.at[k, i], ur.at[k, i], dev)

    def half_rows(a):
        return pl.ds(a * (RB // 2), RB // 2)

    def u_far(k, p):
        if k in X_FIRST:
            n = X_FIRST.index(k)
            src, dst = tb.at[k, zo, 0, xl, half_rows(p)], zf1.at[n, half_rows(p)]
        else:
            n = Z_FIRST.index(k)
            src, dst = tb.at[k, zo, 1 - p], zf.at[n, p]
        return u_copy(k, p, src, dst, d_z[p])

    def u_near(k, p, a):
        slot = (zp, zm)[p]
        if k in X_FIRST:
            n = X_FIRST.index(k)
            src, dst = tb.at[k, slot, 0, xl, half_rows(a)], zs1.at[n, p, half_rows(a)]
        else:
            n = Z_FIRST.index(k)
            src, dst = tb.at[k, slot, a], zn.at[n, p, a]
        return u_copy(k, 2 + 2 * p + a, src, dst, d_z[p])

    def u_xfar(k, p):
        if k in X_FIRST:
            n = X_FIRST.index(k)
            src, dst = tb.at[k, :, 1, xl, half_rows(p)], xf4.at[n, :, half_rows(p)]
        else:
            n = Z_FIRST.index(k)
            src, dst = tb.at[k, z, 1, xl, half_rows(p)], xf.at[n, half_rows(p)]
        return u_copy(k, 6 + p, src, dst, d_x[p])

    def u_xnear(k, p, a):
        if k in X_FIRST:
            n = X_FIRST.index(k)
            src, dst = tb.at[k, :, p, ol, half_rows(a)], xs4.at[n, p, :, half_rows(a)]
        else:
            n = Z_FIRST.index(k)
            src, dst = tb.at[k, z, p, ol, half_rows(a)], xs.at[n, p, half_rows(a)]
        return u_copy(k, 8 + 2 * p + a, src, dst, d_x[p])

    def term(k, h):
        if h == 0:
            t_core(k).wait_recv()
            if k == FIRST0:
                s_core(0).wait_recv()
        elif k == FIRST1:
            s_core(1).wait_recv()

        def tile(j, carry):
            cols = pl.ds(pl.multiple_of(j * 256, 256), 256)
            mine = jnp.concatenate([tg[k, i, c] for i in range(4)], axis=1)
            theirs = jnp.concatenate([tc[k, i] for i in range(4)], axis=1)
            own = slope[own_rows(), cols] if h == 0 else sx[0, :, cols]
            out = jnp.dot(mine, own, preferred_element_type=F32)
            out = out + jnp.dot(theirs, sx[1 + h, :, cols], preferred_element_type=F32)
            tb[k, :, h, :, :, cols] = out.astype(BF).reshape(4, 2, RB, 256)
            return carry

        lax.fori_loop(0, HID // 256, tile, 0)
        if k in Z_FIRST:
            u_far(k, 1 - h).start()
            u_near(k, h, h).start()
        elif h == 1:
            u_xsend(k)

    def u_xsend(k):
        u_xfar(k, 0).start()
        u_xfar(k, 1).start()
        u_xnear(k, 0, 0).start()
        u_xnear(k, 1, 1).start()

    def u_pass(k, p):
        u_far(k, p).wait_recv()
        slot = (zp, zm)[p]
        if k in X_FIRST:
            n = X_FIRST.index(k)
            rows = half_rows(p)
            tb[k, slot, 0, xl, rows] = plus(tb.at[k, slot, 0, xl, rows], zf1.at[n, rows]).astype(BF)
            u_near(k, p, p).start()
        else:
            n = Z_FIRST.index(k)
            tb[k, slot, 1 - p] = plus(tb.at[k, slot, 1 - p], zf.at[n, p]).astype(BF)
            u_near(k, p, 1 - p).start()

    def u_turn(k):
        if k in X_FIRST:
            n = X_FIRST.index(k)
            for p in range(2):
                for a in range(2):
                    u_xnear(k, p, a).wait_recv()
            for i in range(4):
                tb[k, i, 0, xl] = plus(tb.at[k, i, 0, xl], xs4.at[n, 0, i], xs4.at[n, 1, i]).astype(BF)
            u_far(k, 0).start()
            u_far(k, 1).start()
            u_near(k, 0, 1).start()
            u_near(k, 1, 0).start()
        else:
            n = Z_FIRST.index(k)
            for p in range(2):
                for a in range(2):
                    u_near(k, p, a).wait_recv()
            for h, a in ((1, xl), (0, ol), (1, ol)):
                tb[k, z, h, a] = plus(tb.at[k, z, h, a], zn.at[n, 0, h, a], zn.at[n, 1, h, a]).astype(BF)
            u_xsend(k)

    def u_xpass(k, p):
        u_xfar(k, p).wait_recv()
        rows = half_rows(p)
        if k in X_FIRST:
            n = X_FIRST.index(k)
            for i in range(4):
                to = tb.at[k, i, 1 - p, ol, rows]
                to[...] = plus(to, xf4.at[n, i, rows]).astype(BF)
        else:
            n = Z_FIRST.index(k)
            to = tb.at[k, z, 1 - p, ol, rows]
            to[...] = plus(to, xf.at[n, rows]).astype(BF)
        u_xnear(k, 1 - p, p).start()

    def update(k, summed):
        pseudo = summed * (RT * REGIONS) ** (-0.5)
        one = 0.9 * new_first[k] + 0.1 * pseudo
        two = 0.999 * new_second[k] + 0.001 * pseudo * pseudo
        new_mas[k] = new_mas[k] - 0.1 * one / (jnp.sqrt(two) + 0.001)
        new_first[k] = one
        new_second[k] = two

    def u_end(k):
        if k in X_FIRST:
            n = X_FIRST.index(k)
            for p in range(2):
                for a in range(2):
                    u_near(k, p, a).wait_recv()
            update(k, plus(tb.at[k, z, 0, xl], zs1.at[n, 0], zs1.at[n, 1]))
        else:
            n = Z_FIRST.index(k)
            for p in range(2):
                for a in range(2):
                    u_xnear(k, p, a).wait_recv()
            near = zn.at[n, 0, 0, xl], zn.at[n, 1, 0, xl]
            update(k, plus(tb.at[k, z, 0, xl], *near, xs.at[n, 0], xs.at[n, 1]))
        for p in range(2):
            u_far(k, p).wait_send()
            u_xfar(k, p).wait_send()
            for a in range(2):
                u_near(k, p, a).wait_send()
                u_xnear(k, p, a).wait_send()
        t_sent(k)

    def v_far(k, p):
        slot = (oh, xh)[p] * 4 + yo
        return rcopy(ib.at[k, slot], yf.at[k, p], vs.at[k, 1 + p], vr.at[k, 1 + p], d_y[p])

    def v_near(k, p, a):
        slot = (oh, xh)[a] * 4 + (yp, ym)[p]
        i = 3 + 2 * p + a
        return rcopy(ib.at[k, slot], yn.at[k, 2 * p + a], vs.at[k, i], vr.at[k, i], d_y[p])

    def v_last(k):
        return rcopy(ib.at[k, oh * 4 + y], xhb.at[k], vs.at[k, 7], vr.at[k, 7], d_xh)

    def part(k):
        w_core(k, 1 - c).wait_recv()

        def tile(j, carry):
            rows = pl.ds(pl.multiple_of(j * 256, 256), 256)
            left = wg[k].reshape(CD, HID)
            out = lax.dot_general(
                left, slope[rows, :], (((1,), (1,)), ((), ())), preferred_element_type=F32
            )
            out = (out * D ** (-0.5)).astype(BF)
            ib[k, 2 * j] = out[:, :128]
            ib[k, 2 * j + 1] = out[:, 128:]
            return carry

        lax.fori_loop(0, RT // 256, tile, 0)
        v_far(k, 0).start()
        v_far(k, 1).start()
        v_near(k, 0, 1).start()
        v_near(k, 1, 0).start()

    def v_pass(k, p):
        slot = (oh, xh)[p] * 4 + (yp, ym)[p]
        v_far(k, p).wait_recv()
        ib[k, slot] = plus(ib.at[k, slot], yf.at[k, p]).astype(BF)
        v_near(k, p, p).start()

    def v_cross(k):
        v_near(k, 0, 0).wait_recv()
        v_near(k, 1, 0).wait_recv()
        slot = oh * 4 + y
        ib[k, slot] = plus(ib.at[k, slot], yn.at[k, 0], yn.at[k, 2]).astype(BF)
        v_last(k).start()

    def v_end(k):
        v_near(k, 0, 1).wait_recv()
        v_near(k, 1, 1).wait_recv()
        v_last(k).wait_recv()
        ig_out[k] = plus(ib.at[k, s], xhb.at[k], yn.at[k, 1], yn.at[k, 3]).astype(BF)
        v_last(k).wait_send()
        for p in range(2):
            v_far(k, p).wait_send()
            v_near(k, p, 0).wait_send()
            v_near(k, p, 1).wait_send()
        w_sent(k)

    def both(work):
        return lambda k: work(k, 0), lambda k: work(k, 1)

    t_pass0, t_pass1 = both(t_pass)
    u_pass0, u_pass1 = both(u_pass)
    u_xpass0, u_xpass1 = both(u_xpass)
    v_pass0, v_pass1 = both(v_pass)
    term0, term1 = both(term)
    work = {
        T_OWN: t_own, T_PASS0: t_pass0, T_PASS1: t_pass1, T_SHARE: t_share,
        W_OWN: w_own, W_OTHER: w_other, W_PASS0: w_pass0, W_PASS1: w_pass1,
        W_SHARE: w_share, SLOPE0: slope0, SLOPE1: slope1, S_CROSS: s_cross,
        S_PASS: s_pass, TERM0: term0, TERM1: term1, U_PASS0: u_pass0,
        U_PASS1: u_pass1, U_TURN: u_turn, U_XPASS0: u_xpass0, U_XPASS1: u_xpass1,
        U_END: u_end, PART: part, V_PASS0: v_pass0, V_PASS1: v_pass1,
        V_CROSS: v_cross, V_END: v_end,
    }
    waited = ready = False
    for name, k in ORDER:
        if name == W_OWN and not waited:
            get_mas.wait()
            waited = True
        if name == U_END and not ready:
            get_first.wait()
            get_second.wait()
            ready = True
        work[name](k)
    s_sent()


def exchange(tokens, preact, cotangent, master, first, second):
    any_spec = pl.BlockSpec(memory_space=pl.ANY)
    dma = pltpu.SemaphoreType.DMA
    return pl.pallas_call(
        kernel,
        out_shape=(
            pltpu.VMEM((CH, RB, HID), F32),
            pltpu.VMEM((CH, RB, HID), F32),
            pltpu.VMEM((CH, RB, HID), F32),
            pltpu.VMEM((CH, CD, TOK), BF),
        ),
        in_specs=[any_spec] * 6,
        out_specs=(pl.BlockSpec(memory_space=pltpu.VMEM),) * 4,
        scratch_shapes=[
            pltpu.VMEM((CH, 4, 2, HALF, TOK), BF),
            pltpu.VMEM((CH, 4, HALF, TOK), BF),
            pltpu.VMEM((CH, 2, 8, RB, HID), BF),
            pltpu.VMEM((RT, HID), BF),
            pltpu.VMEM((3, HT, HID), BF),
            pltpu.VMEM((CH, 4, 2, 2, RB, HID), BF),
            pltpu.VMEM((len(Z_FIRST), 2, 2, RB, HID), BF),
            pltpu.VMEM((len(Z_FIRST), 2, 2, 2, RB, HID), BF),
            pltpu.VMEM((len(Z_FIRST), RB, HID), BF),
            pltpu.VMEM((len(Z_FIRST), 2, RB, HID), BF),
            pltpu.VMEM((len(X_FIRST), 4, RB, HID), BF),
            pltpu.VMEM((len(X_FIRST), 2, 4, RB, HID), BF),
            pltpu.VMEM((len(X_FIRST), RB, HID), BF),
            pltpu.VMEM((len(X_FIRST), 2, RB, HID), BF),
            pltpu.VMEM((CH, SEQS, CD, TOK), BF),
            pltpu.VMEM((CH, 2, CD, TOK), BF),
            pltpu.VMEM((CH, 4, CD, TOK), BF),
            pltpu.VMEM((CH, CD, TOK), BF),
            pltpu.VMEM((TOK, D), BF),
            pltpu.VMEM((2, STAGE, HID), BF),
            pltpu.VMEM((2, STAGE, HID), BF),
            dma((4,)),
            dma((2, 2)),
            dma((CH, 5)),
            dma((CH, 5)),
            dma((CH, 8)),
            dma((CH, 8)),
            dma((CH, 12)),
            dma((CH, 12)),
            dma((CH, 8)),
            dma((CH, 8)),
            dma((6,)),
            dma((6,)),
        ],
        compiler_params=pltpu.CompilerParams(
            collective_id=0, has_side_effects=True, vmem_limit_bytes=55 * 2**20
        ),
        cost_estimate=pl.CostEstimate(
            flops=4 * RT * HID * D, bytes_accessed=12 * 2**20, transcendentals=RT * HID
        ),
        name="exchange",
    )(tokens, preact, cotangent, master, first, second)


def finish_kernel(a, b, c, turned, new_a, new_b, new_c, grad, gradv, sems):
    puts = [pltpu.make_async_copy(src, dst, sems.at[i]) for i, (src, dst) in enumerate(((a, new_a), (b, new_b), (c, new_c)))]
    for copy in puts:
        copy.start()
    for j in range(D // 128):
        pieces = []
        for m in range(128 // RB):
            q, row = place(j * 128 + m * RB)
            pieces.append(turned[q, row:row + RB, :])
        gradv[:, j * 128:(j + 1) * 128] = jnp.concatenate(pieces, axis=0).T
    puts.append(pltpu.make_async_copy(gradv, grad, sems.at[3]))
    puts[3].start()
    for copy in puts:
        copy.wait()


def finish(*results):
    state = jax.ShapeDtypeStruct((CH, RB, HID), F32)
    return pl.pallas_call(
        finish_kernel,
        out_shape=(state, state, state, jax.ShapeDtypeStruct((TOK, D), BF)),
        in_specs=[pl.BlockSpec(memory_space=pltpu.VMEM)] * 4,
        out_specs=(pl.BlockSpec(memory_space=pl.ANY),) * 4,
        scratch_shapes=[pltpu.VMEM((TOK, D), BF), pltpu.SemaphoreType.DMA((4,))],
        compiler_params=pltpu.CompilerParams(vmem_limit_bytes=16 * 2**20),
        name="finish",
    )(*results)


def per_device(tokens, preact, cotangent, master, first_moment, second_moment):
    states = [x.reshape(CH, RB, HID) for x in (master, first_moment, second_moment)]
    *new, grad = finish(*exchange(tokens, preact, cotangent, *states))
    return (*[x.reshape(OWN, HID) for x in new], grad)


def solution(mesh):
    block = P("region", "seq")
    rows = P(("region", "seq"), None)
    return jax.shard_map(
        per_device,
        mesh=mesh,
        in_specs=(rows, block, block, block, block, block),
        out_specs=(block, block, block, rows),
        check_vma=False,
    )
```
